512 devices in a mesh: sec: 2 (over core), ep: 64 (over z, y), tp: 4 (over x).
Axes of the slice: x: 4, y: 8, z: 8, core: 2. Of those that a mesh axis runs over, the one named last changes fastest.
Arguments:
- resid: bfloat16 [16384, 4096], P(('sec', 'ep'), 'tp'), may hold values from -6 to 6
- queries: bfloat16 [16384, 4096], P(('sec', 'ep'), 'tp'), may hold values from -48 to 48
- keys: bfloat16 [16384, 4096], P(('sec', 'ep'), 'tp'), may hold values from -6 to 6
- values: bfloat16 [16384, 4096], P(('sec', 'ep'), 'tp'), may hold values from -6 to 6
- norm_gain: float32 [4096], P('tp'), may hold values from 0.25 to 1.75
- w_router: float32 [4096, 64], P('tp'), may hold values from -0.09375 to 0.09375
- expert_ids: int32 [16384, 2], P(('sec', 'ep')), may hold values from 0 to 63, all different within a row; in each aligned block of 128 rows (0 to 127, 128 to 255, ...) at most 8 rows name the same one
- w_gate: bfloat16 [64, 4096, 1024], P('ep', 'sec', 'tp'), may hold values from -0.09375 to 0.09375
- w_up: bfloat16 [64, 4096, 1024], P('ep', 'sec', 'tp'), may hold values from -0.09375 to 0.09375
- w_down: bfloat16 [64, 1024, 4096], P('ep', 'tp', 'sec'), may hold values from -0.1875 to 0.1875
Outputs:
- mixed: bfloat16 [16384, 4096], P(('sec', 'ep'), 'tp')
The draws below stay inside these ranges and needn't reach their ends.
Inputs may be any that keep to these rules, and one draw needn't show every extreme that they name: `expert_ids`: the two ids of a token differ. Among the 128 tokens of one device (aligned blocks of 128 rows) no expert is picked more than 8 times.
All inputs are finite; a program needn't handle non-finite values.
Results may differ from the reference program's by a relative error of at most 0.015.
Values may be sent and summed in bfloat16 or wider, within the bound.
No kernel may reach another device: no remote copies, remote signals or barrier semaphores. Data moves between devices by JAX's collectives and lax.ppermute only.
A program may use at most 64 MiB of HBM per device.

```python
import math
import jax
import jax.numpy as jnp
import numpy as np
from jax import lax

D = 4096
HEADS = 32
HEAD_DIM = 128
FF = 1024
WINDOW = 128
TOK_DEV = 128
EXPERTS = 64
CAP = 8
TOKENS = 16384
N_TP = 4


def draw_queries(key, part):
    key = jax.random.fold_in(key, 11)
    result = jnp.clip(jax.random.normal(key, (TOKENS, D), jnp.float32), -6.0, 6.0)
    return result.astype(jnp.bfloat16)


def draw_keys(key, part):
    key = jax.random.fold_in(key, 12)
    result = jnp.clip(jax.random.normal(key, (TOKENS, D), jnp.float32), -6.0, 6.0)
    return result.astype(jnp.bfloat16)


def block_scale(rng, extent, pieces, low, largest):
    factor_of = 1.0
    for position, parts in pieces:
        steps = jax.random.uniform(jax.random.fold_in(jax.random.fold_in(rng, 6), position), (parts,), jnp.float32, low / len(pieces), largest / len(pieces))
        factor_of = factor_of * jnp.repeat(jnp.exp(steps), extent[position] // parts).reshape((-1,) + (1,) * (len(extent) - 1 - position))
    return factor_of


def shared_out(rng, own, number, rows, count, top, limit, skew):
    order = jax.random.permutation(rng, count)
    packed, common = portions_of(count, rows * top, limit, skew, True), portions_of(count, rows * top, limit, skew, False)
    places = jnp.arange(count)

    def named(sizes, turn):
        used = int((sizes > 0).sum())
        fixed = max(1, used // 4)
        shifted = fixed + (places - fixed + turn * (used - fixed)) % max(1, count - fixed)
        return jnp.zeros((count,), jnp.int32).at[order[jnp.where(places < fixed, places, shifted)]].set(jnp.asarray(sizes, jnp.int32))

    sizes = jnp.where(number % 4 == 0, named(packed, number // 4), named(common, number - number // 4 - 1))
    mixed = jax.random.permutation(jax.random.fold_in(own, 3), count)
    donor, receiver = mixed[0:count // 2 * 2:2], mixed[1:count // 2 * 2:2]
    slack = jnp.minimum(sizes[donor] - 1, limit - sizes[receiver]) // 2
    slack = jnp.where((donor == order[0]) | (receiver == order[0]) | (sizes[receiver] == 0), 0, jnp.maximum(slack, 0))
    shifted = jax.random.randint(jax.random.fold_in(own, 4), (count // 2,), 0, 1 << 20) % (slack + 1)
    sizes = sizes.at[donor].add(-shifted).at[receiver].add(shifted)
    members = jnp.searchsorted(jnp.cumsum(sizes), jnp.arange(rows * top), side="right").astype(jnp.int32)
    listing = members.reshape(top, rows).T
    listing = listing[jax.random.permutation(jax.random.fold_in(own, 1), rows)]
    turn = jax.random.randint(jax.random.fold_in(own, 2), (rows, 1), 0, top)
    return jnp.take_along_axis(listing, (jnp.arange(top)[None, :] + turn) % top, axis=1)


def portions_of(number_of, total, limit, lean, full):
    portions = [(1 << 20) // math.isqrt(rank ** lean) + 1 for rank in range(1, number_of + 1)]
    largest = limit if full else min(limit, max(-(-total // number_of), total * portions[0] // sum(portions)))
    least = 1 if total - largest >= number_of - 1 else 0
    given, spare = [largest] + [least] * (number_of - 1), total - largest - least * (number_of - 1)
    while spare > 0:
        movable = [i for i in range(1, number_of) if given[i] < largest] or [i for i in range(1, number_of) if given[i] < limit]
        whole, budget = sum([portions[i] for i in movable]), spare
        for i in movable:
            addition = min(limit - given[i], max(1, budget * portions[i] // whole), spare)
            given[i] = given[i] + addition
            spare = spare - addition
    return np.array(given)


def centred(key, extent, scale, limit, cuts=(), held_as=jnp.bfloat16):
    loudness = block_scale(key, extent, cuts, -0.22, 0.18) if cuts else 1.0
    entries = jax.random.normal(key, extent, jnp.float32) * scale * loudness
    return jnp.minimum(jnp.maximum(entries, -limit), limit).astype(held_as)


def setup_inputs(seed: int = 0) -> dict:
    seeds = jax.random.split(jax.random.key(seed), 11)
    resid = centred(seeds[0], (TOKENS, D), 1.0, 6.0, ((0, 128), (1, 4)))
    queries = draw_queries(jax.random.fold_in(seeds[10], 71), 0)
    keys = draw_keys(jax.random.fold_in(seeds[10], 71), 0)
    values = centred(seeds[3], (TOKENS, D), 1.0, 6.0, ((0, 128), (1, 4)))
    norm_gain = jnp.clip(1.0 + 0.15 * jax.random.normal(seeds[4], (D,), jnp.float32), 0.25, 1.75)
    w_router = centred(seeds[5], (D, EXPERTS), D ** -0.5, 0.09375, ((0, 4),), jnp.float32)
    expert_ids_keys = jax.random.split(jax.random.fold_in(seeds[6], 1), TOKENS // TOK_DEV)
    expert_ids_turns = jax.random.permutation(jax.random.fold_in(seeds[6], 3), TOKENS // TOK_DEV)
    expert_ids = jax.vmap(lambda own, number: shared_out(jax.random.fold_in(seeds[6], 2), own, number, TOK_DEV, EXPERTS, 2, CAP, 2))(expert_ids_keys, expert_ids_turns).reshape((TOKENS, 2))
    w_gate = centred(seeds[7], (EXPERTS, D, FF), D ** -0.5, 0.09375, ((0, 64), (1, 2), (2, 4)))
    w_up = centred(seeds[8], (EXPERTS, D, FF), D ** -0.5, 0.09375, ((0, 64), (1, 2), (2, 4)))
    w_down = centred(seeds[9], (EXPERTS, FF, D), FF ** -0.5, 0.1875, ((0, 64), (1, 4), (2, 2)))
    return dict(resid=resid, queries=queries, keys=keys, values=values, norm_gain=norm_gain, w_router=w_router, expert_ids=expert_ids, w_gate=w_gate, w_up=w_up, w_down=w_down)


epsilon = 1e-06

def reference(resid, queries, keys, values, norm_gain, w_router, expert_ids, w_gate, w_up, w_down):
    windows = TOKENS // WINDOW
    query_blocks = queries.astype(jnp.float32).reshape(windows, WINDOW, HEADS, HEAD_DIM)
    key_blocks = keys.astype(jnp.float32).reshape(windows, WINDOW, HEADS, HEAD_DIM)
    value_blocks = values.astype(jnp.float32).reshape(windows, WINDOW, HEADS, HEAD_DIM)
    scores = jnp.einsum('wqhd,wkhd->whqk', query_blocks, key_blocks) / math.sqrt(HEAD_DIM)
    attn_weights = jax.nn.softmax(scores, axis=-1).astype(jnp.bfloat16)
    attended = jnp.einsum('whqk,wkhd->wqhd', attn_weights.astype(jnp.float32), value_blocks).reshape(TOKENS, D)
    hidden_state = (resid.astype(jnp.float32) + attended).astype(jnp.bfloat16)
    hidden_f32 = hidden_state.astype(jnp.float32)
    gain_f32 = norm_gain.astype(jnp.float32)
    inv_rms = lax.rsqrt(lax.optimization_barrier(jnp.mean(hidden_f32 * hidden_f32, axis=1, keepdims=True)) + epsilon)
    normed = (hidden_f32 * inv_rms * gain_f32).astype(jnp.bfloat16)
    logits = inv_rms * jnp.dot(hidden_f32 * gain_f32, w_router.astype(jnp.float32), precision=lax.Precision.HIGHEST)
    affinity = jax.nn.sigmoid(logits)
    expert_range = jnp.arange(EXPERTS, dtype=jnp.int32)
    picked = lax.optimization_barrier(jnp.sum(jnp.where(expert_ids[:, :, None] == expert_range[None, None, :], affinity[:, None, :], 0.0), axis=2))
    gate_share = picked / lax.optimization_barrier(jnp.sum(picked, axis=1, keepdims=True))
    blocks = TOKENS // TOK_DEV
    flat_ids = expert_ids.reshape(blocks, TOK_DEV * 2).astype(jnp.int32)
    onehot = (flat_ids[:, :, None] == expert_range[None, None, :]).astype(jnp.int32)
    rank_in_block = lax.optimization_barrier(jnp.sum((jnp.cumsum(onehot, axis=1) - 1) * onehot, axis=2))
    block_base = jnp.arange(blocks, dtype=jnp.int32)[:, None] * CAP
    slot_index = (flat_ids * (blocks * CAP) + block_base + rank_in_block).reshape(-1).astype(jnp.int32)
    pair_rows = jnp.repeat(normed, 2, axis=0)
    buffer = jnp.zeros((EXPERTS * blocks * CAP, D), jnp.bfloat16).at[slot_index].set(pair_rows)
    buffer = buffer.reshape(EXPERTS, blocks * CAP, D)
    block_units = FF // N_TP

    def expert(operands):
        expert_rows, gate_mat, up_mat, down_mat = operands
        gate_proj = jnp.dot(expert_rows, gate_mat, preferred_element_type=jnp.float32)
        up_proj = jnp.dot(expert_rows, up_mat, preferred_element_type=jnp.float32)
        inner_act = (jax.nn.silu(gate_proj) * up_proj).astype(jnp.bfloat16)
        total = jnp.zeros((expert_rows.shape[0], D), jnp.float32)
        for piece_no in range(N_TP):
            lower = piece_no * block_units
            part_sum = jnp.dot(inner_act[:, lower:lower + block_units], down_mat[lower:lower + block_units], preferred_element_type=jnp.float32)
            rounded = lax.optimization_barrier(part_sum.astype(jnp.bfloat16))
            total = total + rounded.astype(jnp.float32)
        return total.astype(jnp.bfloat16)
    outputs = lax.map(expert, (buffer, w_gate, w_up, w_down))
    picked_rows = outputs.reshape(EXPERTS * blocks * CAP, D)[slot_index].reshape(TOKENS, 2, D).astype(jnp.float32)
    mixed = hidden_f32 + lax.optimization_barrier(jnp.sum(gate_share[:, :, None] * picked_rows, axis=1))
    return mixed.astype(jnp.bfloat16)
```

```python
import math

import jax
import jax.numpy as jnp
from jax import lax
from jax.experimental import pallas as pl
from jax.experimental.pallas import tpu as pltpu
from jax.sharding import PartitionSpec as P

D = 4096
HEAD_DIM = 128
CAP = 8
N_TP = 4
EPS = 1e-06

BF = jnp.bfloat16
F32 = jnp.float32
HIGHEST = lax.Precision.HIGHEST
VMEM_BYTES = 48 * 1024 * 1024


def call(kernel, out_shape, in_specs, scratch=(), cost=None, single=True):
    out_specs = jax.tree.map(lambda s: pl.BlockSpec(memory_space=pltpu.VMEM), out_shape)
    if not single:
        out_specs = jax.tree.map(lambda s: pl.BlockSpec(memory_space=pl.ANY), out_shape)
    return pl.pallas_call(
        kernel,
        out_shape=out_shape,
        in_specs=in_specs,
        out_specs=out_specs,
        scratch_shapes=scratch,
        cost_estimate=cost,
        compiler_params=pltpu.CompilerParams(vmem_limit_bytes=VMEM_BYTES),
    )


VM = pl.BlockSpec(memory_space=pltpu.VMEM)
ANY = pl.BlockSpec(memory_space=pl.ANY)
SM = pl.BlockSpec(memory_space=pltpu.SMEM)


def struct(shape, dtype):
    return jax.ShapeDtypeStruct(shape, dtype)


def nt(a, b, precision=None):
    return lax.dot_general(
        a, b, (((1,), (1,)), ((), ())), precision=precision, preferred_element_type=F32
    )


def pack_kernel(parity, gate, up, down, first, second, sems):
    width = gate.shape[2]
    span = down.shape[2] // 2
    copies = []
    for turn, out in enumerate((first, second)):
        block = parity[0] if turn == 0 else 1 - parity[0]
        base = block * span
        for j in range(span // width):
            rows = pl.ds(pl.multiple_of(base + j * width, width), width)
            cols = pl.ds(j * width, width)
            copies.append((gate.at[0, rows, :], out.at[pl.ds(0, width), cols]))
            copies.append((up.at[0, rows, :], out.at[pl.ds(width, width), cols]))
        cols = pl.ds(pl.multiple_of(base, span), span)
        copies.append((down.at[0, :, cols], out.at[pl.ds(2 * width, width), :]))
    started = [
        pltpu.make_async_copy(src, dst, sems.at[n]) for n, (src, dst) in enumerate(copies)
    ]
    for copy in started:
        copy.start()
    for copy in started:
        copy.wait()


def slots_of(ids_ref, experts):
    tokens = ids_ref.shape[1]
    expert = lax.broadcasted_iota(jnp.int32, (experts, tokens), 0)
    named = (ids_ref[0:1, :] == expert) | (ids_ref[1:2, :] == expert)
    before = lax.broadcasted_iota(jnp.int32, (tokens, tokens), 0) < lax.broadcasted_iota(
        jnp.int32, (tokens, tokens), 1
    )
    rank = jnp.dot(named.astype(BF), before.astype(BF), preferred_element_type=F32)
    return named, jnp.where(named, rank, -1.0)


def spread(slot, value):
    experts, tokens = slot.shape
    turn = lax.broadcasted_iota(jnp.int32, (experts, CAP, tokens), 1).astype(F32)
    hit = slot[:, None, :] == turn
    return jnp.where(hit, value[:, None, :], 0.0).reshape(experts * CAP, tokens)


def attention_kernel(experts, ids, q, k, v, resid, hidden, outgoing):
    tokens, width = q.shape
    scale = 1.0 / math.sqrt(HEAD_DIM)
    _, slot = slots_of(ids, experts)
    pick = spread(slot, jnp.ones_like(slot)).astype(BF)
    for n in range(width // HEAD_DIM):
        cols = slice(n * HEAD_DIM, (n + 1) * HEAD_DIM)
        scores = nt(q[:, cols], k[:, cols]) * scale
        top = jnp.max(scores, axis=1, keepdims=True)
        e = jnp.exp(scores - top)
        weights = (e / jnp.sum(e, axis=1, keepdims=True)).astype(BF)
        attended = jnp.dot(weights, v[:, cols], preferred_element_type=F32)
        h = (resid[:, cols].astype(F32) + attended).astype(BF)
        hidden[:, cols] = h
        outgoing[:, cols] = jnp.dot(pick, h, preferred_element_type=F32).astype(BF)


def router_kernel(hidden, gain, router, out):
    h = hidden[...].astype(F32)
    experts = router.shape[0]
    out[0:experts, :] = nt(router[...], h * gain[...], HIGHEST)
    out[experts : experts + 8, :] = nt(jnp.ones((8, h.shape[1]), F32), h * h, HIGHEST)


def pick_block(flag, mine, other, n):
    return (mine[n % 2], other[n % 2]) if n < 2 else (other[n % 2], mine[n % 2])


def up_kernel(flag, x, gain, u0, u1, v0, v1, own, own_square, s1, s2, s3, weights, sems):
    rows, depth = x.shape
    width = u0.shape[0] // 3
    order = (2, 1, 3, 0)

    def copy(n, ref):
        return pltpu.make_async_copy(ref.at[pl.ds(0, 2 * width), :], weights.at[n], sems.at[n])

    for n in order:
        yes, no = pick_block(flag, (u0, u1), (v0, v1), n)

        @pl.when(flag[0] == 1)
        def _():
            copy(n, yes).start()

        @pl.when(flag[0] != 1)
        def _():
            copy(n, no).start()

    xf = x[...].astype(F32)
    xg = (xf * gain[...]).astype(BF)
    square = xf * xf
    high = square.astype(BF)
    low = (square - high.astype(F32)).astype(BF)
    ones = jnp.ones((8, depth), BF)
    total = nt(ones, high) + nt(ones, low)
    own_square[...] = total
    t_high = total.astype(BF)
    t_low = (total - t_high.astype(F32)).astype(BF)
    sums = jnp.concatenate([t_high, t_low], axis=0)
    for n in order:
        copy(n, u0).wait()
        gate = jnp.zeros((rows, width), F32)
        up = jnp.zeros((rows, width), F32)
        for j in range(depth // width):
            cols = slice(j * width, (j + 1) * width)
            part = xg[:, cols]
            gate += jnp.dot(part, weights[n, 0:width, cols], preferred_element_type=F32)
            up += jnp.dot(part, weights[n, width : 2 * width, cols], preferred_element_type=F32)
        if n == 0:
            own[:, 0:width] = gate
            own[:, width : 2 * width] = up
        else:
            out = (s1, s2, s3)[n - 1]
            out[0:rows, 0:width] = gate.astype(BF)
            out[0:rows, width : 2 * width] = up.astype(BF)
            out[rows : rows + 16, :] = sums


def inner_kernel(own, own_square, r1, r2, r3, inner):
    rows, width2 = own.shape
    width = width2 // 2
    square = own_square[...]
    total = own[...]
    for r in (r1, r2, r3):
        sums = r[rows : rows + 16, :].astype(F32)
        square = square + sums[0:8, :] + sums[8:16, :]
        total = total + r[0:rows, :].astype(F32)
    inv = lax.rsqrt(square[0:1, :] / D + EPS)
    for j in range(rows // 128):
        part = slice(j * 128, (j + 1) * 128)
        column = jnp.transpose(jnp.broadcast_to(inv[:, part], (128, 128)), (1, 0))
        column = jnp.concatenate([column] * (width // 128), axis=1)
        gate = total[part, 0:width] * column
        up = total[part, width : 2 * width] * column
        inner[part, :] = (gate * (1.0 / (1.0 + jnp.exp(-gate))) * up).astype(BF)


def down_kernel(flag, i0, i1, i2, i3, u0, u1, v0, v1, out, weights, sems):
    width = u0.shape[0] // 3
    order = (0, 1, 2, 3)

    def copy(n, ref):
        return pltpu.make_async_copy(
            ref.at[pl.ds(2 * width, width), :], weights.at[pl.ds(n * width, width), :], sems.at[n]
        )

    for n in order:
        yes, no = pick_block(flag, (u0, u1), (v0, v1), n)

        @pl.when(flag[0] == 1)
        def _():
            copy(n, yes).start()

        @pl.when(flag[0] != 1)
        def _():
            copy(n, no).start()

    for n in order:
        copy(n, u0).wait()
    inner = jnp.concatenate([i0[...], i1[...], i2[...], i3[...]], axis=1)
    out[...] = jnp.dot(inner, weights[...], preferred_element_type=F32).astype(BF)


def mix_kernel(ids, sums, hidden, returned, out):
    experts = sums.shape[0] - 8
    named, slot = slots_of(ids, experts)
    inv = lax.rsqrt(sums[experts : experts + 1, :] / D + EPS)
    logits = sums[0:experts, :] * inv
    picked = jnp.where(named, 1.0 / (1.0 + jnp.exp(-logits)), 0.0)
    share = picked / jnp.sum(picked, axis=0, keepdims=True)
    wide = spread(slot, share)
    high = wide.astype(BF)
    low = (wide - high.astype(F32)).astype(BF)
    rows = returned[...]
    dims = (((0,), (0,)), ((), ()))
    mixed = lax.dot_general(high, rows, dims, preferred_element_type=F32)
    mixed += lax.dot_general(low, rows, dims, preferred_element_type=F32)
    out[...] = (hidden[...].astype(F32) + mixed).astype(BF)


def body(resid, queries, keys, values, norm_gain, w_router, expert_ids, w_gate, w_up, w_down):
    tokens, width = resid.shape
    experts = lax.axis_size("ep")
    slots = experts * CAP
    units = w_gate.shape[2]
    sec, tp = lax.axis_index("sec"), lax.axis_index("tp")
    parity = (tp % 2).astype(jnp.int32).reshape(1)
    flag = (sec == tp // 2).astype(jnp.int32).reshape(1)
    ids = expert_ids.T
    gain = norm_gain.reshape(1, width)

    payload = struct((3 * units, width), BF)
    first, second = call(
        pack_kernel,
        [payload, payload],
        [SM, ANY, ANY, ANY],
        [pltpu.SemaphoreType.DMA((18,))],
        single=False,
    )(parity, w_gate, w_up, w_down)
    stay, turn = [], []
    for s in range(2):
        for t in range(N_TP):
            here = s * N_TP + t
            if s == t // 2:
                stay.append((here, here))
            else:
                stay.append((here, (1 - s) * N_TP + (t + 2) % N_TP))
            if s == ((t + 1) % N_TP) // 2:
                turn.append((here, s * N_TP + (t + 1) % N_TP))
            else:
                turn.append((here, (1 - s) * N_TP + (t + 3) % N_TP))
    u0 = lax.ppermute(first, ("sec", "tp"), stay)
    u1 = lax.ppermute(second, ("sec", "tp"), turn)
    swap = [(0, 1), (1, 0)]
    v0 = lax.ppermute(u0, "sec", swap)
    v1 = lax.ppermute(u1, "sec", swap)

    hidden, outgoing = call(
        lambda *refs: attention_kernel(experts, *refs),
        [struct((tokens, width), BF), struct((slots, width), BF)],
        [VM] * 5,
        cost=pl.CostEstimate(flops=300_000_000, bytes_accessed=2_500_000, transcendentals=131072),
    )(ids, queries, keys, values, resid)
    arrived = lax.all_to_all(
        outgoing.reshape(experts, CAP, width), "ep", split_axis=0, concat_axis=0, tiled=True
    ).reshape(slots, width)

    sums = call(
        router_kernel, struct((experts + 8, tokens), F32), [VM] * 3,
        cost=pl.CostEstimate(flops=150_000_000, bytes_accessed=600_000, transcendentals=0),
    )(hidden, gain, w_router.T)
    sums = lax.psum(sums, "tp")

    message = struct((slots + 16, 2 * units), BF)
    own, own_square, *outs = call(
        up_kernel,
        [struct((slots, 2 * units), F32), struct((8, slots), F32), message, message, message],
        [SM, VM, VM, ANY, ANY, ANY, ANY],
        [pltpu.VMEM((N_TP, 2 * units, width), BF), pltpu.SemaphoreType.DMA((N_TP,))],
        cost=pl.CostEstimate(flops=2_200_000_000, bytes_accessed=8_000_000, transcendentals=0),
    )(flag, arrived, gain, u0, u1, v0, v1)
    got = [None] * N_TP
    for k in (2, 1, 3):
        got[k] = lax.ppermute(outs[k - 1], "tp", [(i, (i - k) % N_TP) for i in range(N_TP)])
    inner = call(inner_kernel, struct((slots, units), BF), [VM] * 5)(
        own, own_square, got[1], got[2], got[3]
    )
    inners = [inner] + [None] * 3
    for k in (2, 1, 3):
        inners[k] = lax.ppermute(inner, "tp", [(i, (i + k) % N_TP) for i in range(N_TP)])
    partial = call(
        down_kernel,
        struct((slots, width), BF),
        [SM, VM, VM, VM, VM, ANY, ANY, ANY, ANY],
        [pltpu.VMEM((N_TP * units, width), BF), pltpu.SemaphoreType.DMA((N_TP,))],
        cost=pl.CostEstimate(flops=1_100_000_000, bytes_accessed=4_000_000, transcendentals=0),
    )(flag, *inners, u0, u1, v0, v1)
    returned = lax.all_to_all(
        partial.reshape(experts, CAP, width), "ep", split_axis=0, concat_axis=0, tiled=True
    ).reshape(slots, width)
    return call(mix_kernel, struct((tokens, width), BF), [VM] * 4)(ids, sums, hidden, returned)


def solution(mesh):
    rows, cols = P(("sec", "ep"), "tp"), P(("sec", "ep"), None)
    return jax.shard_map(
        body,
        mesh=mesh,
        in_specs=(
            rows,
            rows,
            rows,
            rows,
            P("tp"),
            P("tp", None),
            cols,
            P("ep", "sec", "tp"),
            P("ep", "sec", "tp"),
            P("ep", "tp", "sec"),
        ),
        out_specs=rows,
        check_vma=False,
    )
```

```python
import math

import jax
import jax.numpy as jnp
from jax import lax
from jax.experimental import pallas as pl
from jax.experimental.pallas import tpu as pltpu
from jax.sharding import PartitionSpec as P

D = 4096
HEAD_DIM = 128
CAP = 8
N_TP = 4
EPS = 1e-06

BF = jnp.bfloat16
F32 = jnp.float32
HIGHEST = lax.Precision.HIGHEST
VMEM_BYTES = 48 * 1024 * 1024
WHOLE_VMEM = 63 * 1024 * 1024


def call(kernel, out_shape, in_specs, out_specs, scratch=(), cost=(0, 0), vmem=VMEM_BYTES):
    return pl.pallas_call(
        kernel,
        out_shape=out_shape,
        in_specs=in_specs,
        out_specs=out_specs,
        scratch_shapes=scratch,
        cost_estimate=pl.CostEstimate(flops=cost[0], bytes_accessed=cost[1], transcendentals=0),
        compiler_params=pltpu.CompilerParams(vmem_limit_bytes=vmem),
    )


VM = pl.BlockSpec(memory_space=pltpu.VMEM)
ANY = pl.BlockSpec(memory_space=pl.ANY)
SM = pl.BlockSpec(memory_space=pltpu.SMEM)


def struct(shape, dtype):
    return jax.ShapeDtypeStruct(shape, dtype)


def nt(a, b, precision=None):
    return lax.dot_general(
        a, b, (((1,), (1,)), ((), ())), precision=precision, preferred_element_type=F32
    )


def pack_kernel(block, gate, up, down, *rest):
    out, sems = rest[-2:]
    width = gate.shape[2]
    span = down.shape[2] // 2
    base = pl.multiple_of(block[0] * span, span)
    rows = pl.ds(base, span)
    copies = [
        (gate.at[0, rows, :], out.at[pl.ds(0, span), pl.ds(0, width)]),
        (up.at[0, rows, :], out.at[pl.ds(0, span), pl.ds(width, width)]),
    ]
    for j in range(2):
        cols = pl.ds(pl.multiple_of(base + j * 2 * width, 2 * width), 2 * width)
        copies.append((down.at[0, :, cols], out.at[pl.ds(span + j * width, width), :]))
    started = [
        pltpu.make_async_copy(src, dst, sems.at[n]) for n, (src, dst) in enumerate(copies)
    ]
    for copy in started:
        copy.start()
    for copy in started:
        copy.wait()


def slots_of(ids_ref, experts):
    tokens = ids_ref.shape[1]
    expert = lax.broadcasted_iota(jnp.int32, (experts, tokens), 0)
    named = (ids_ref[0:1, :] == expert) | (ids_ref[1:2, :] == expert)
    before = lax.broadcasted_iota(jnp.int32, (tokens, tokens), 0) < lax.broadcasted_iota(
        jnp.int32, (tokens, tokens), 1
    )
    rank = jnp.dot(named.astype(BF), before.astype(BF), preferred_element_type=F32)
    return named, jnp.where(named, rank, -1.0)


def spread(slot, value):
    experts, tokens = slot.shape
    turn = lax.broadcasted_iota(jnp.int32, (experts, CAP, tokens), 1).astype(F32)
    hit = slot[:, None, :] == turn
    return jnp.where(hit, value[:, None, :], 0.0).reshape(experts * CAP, tokens)


def attention_kernel(experts, ids, q, k, v, resid, hidden, outgoing, rows, sems):
    tokens, width = q.shape
    scale = 1.0 / math.sqrt(HEAD_DIM)
    _, slot = slots_of(ids, experts)
    pick = spread(slot, jnp.ones_like(slot)).astype(BF)
    copies = []
    for n in range(width // HEAD_DIM):
        cols = slice(n * HEAD_DIM, (n + 1) * HEAD_DIM)
        scores = nt(q[:, cols], k[:, cols]) * scale
        top = jnp.max(scores, axis=1, keepdims=True)
        e = jnp.exp(scores - top)
        weights = (e / jnp.sum(e, axis=1, keepdims=True)).astype(BF)
        attended = jnp.dot(weights, v[:, cols], preferred_element_type=F32)
        h = (resid[:, cols].astype(F32) + attended).astype(BF)
        hidden[:, cols] = h
        rows[:, cols] = jnp.dot(pick, h, preferred_element_type=F32).astype(BF)
        if n % 2 == 1:
            pair = pl.ds((n - 1) * HEAD_DIM, 2 * HEAD_DIM)
            copies.append(
                pltpu.make_async_copy(rows.at[:, pair], outgoing.at[:, pair], sems.at[n // 2])
            )
            copies[-1].start()
    for copy in copies:
        copy.wait()


def router_kernel(hidden, gain, router, out):
    h = hidden[...].astype(F32)
    experts = router.shape[0]
    out[0:experts, :] = nt(router[...], h * gain[...], HIGHEST)
    out[experts : experts + 8, :] = nt(jnp.ones((8, h.shape[1]), F32), h * h, HIGHEST)


def fetch(flag, mine, other, copies_of, nblocks):
    for n in range(nblocks):
        refs = (mine[n % 2], other[n % 2])

        @pl.when(flag[0] == (1 if n < 2 else 0))
        def _():
            for copy in copies_of(n, refs[0]):
                copy.start()

        @pl.when(flag[0] != (1 if n < 2 else 0))
        def _():
            for copy in copies_of(n, refs[1]):
                copy.start()


def split(value):
    high = value.astype(BF)
    return high, (value - high.astype(F32)).astype(BF)


def up_kernel(place, x, gain, sums, u0, u1, v0, v1, out, weights, made, sems, out_sems):
    rows, depth = x.shape
    order = (2, 1, 3, 0)

    def copies_of(n, ref):
        return [pltpu.make_async_copy(ref.at[pl.ds(0, depth), :], weights.at[n], sems.at[n])]

    fetch(place, (u0, u1), (v0, v1), copies_of, N_TP)
    xf = x[...].astype(F32)
    xg = (xf * gain[...]).astype(BF)
    high, low = split(xf * xf)
    ones = jnp.ones((8, depth), BF)
    total = nt(ones, high) + nt(ones, low)
    experts = sums.shape[0] - 8
    tokens = jnp.concatenate([sums[experts : experts + 8, :]] * 4, axis=1)
    tile = lax.broadcasted_iota(jnp.int32, total.shape, 0)
    squares = jnp.concatenate(split(jnp.where(tile < 4, total, tokens)), axis=0)
    half = experts // 2
    parts = split(sums[0:experts, :])
    logits = jnp.concatenate([part[i * half : (i + 1) * half, :] for part in parts for i in range(2)], axis=1)
    done = []
    for n in order:
        copies_of(n, u0)[0].wait()
        made[n, 0:rows, :] = jnp.dot(xg, weights[n], preferred_element_type=F32).astype(BF)
        made[n, rows : rows + 16, :] = squares
        made[n, rows + 16 : rows + 16 + half, :] = logits
        done.append(pltpu.make_async_copy(made.at[n], out.at[place[1 + n]], out_sems.at[n]))
        done[-1].start()
    for copy in done:
        copy.wait()


def inner_kernel(got, inner, sums):
    rows, width = inner.shape
    half = sums.shape[0] // 2 - 4
    total = got[0, 0:rows, :].astype(F32)
    tail = got[0, rows:, :].astype(F32)
    for n in range(1, N_TP):
        total = total + got[n, 0:rows, :].astype(F32)
        tail = tail + got[n, rows:, :].astype(F32)
    square = tail[0:8, :] + tail[8:16, :]
    logits = tail[16 : 16 + half, :]
    logits = logits[:, 0:256] + logits[:, 256:512]
    sums[0:half, :] = logits[:, 0:128]
    sums[half : 2 * half, :] = logits[:, 128:256]
    sums[2 * half : 2 * half + 8, :] = jnp.broadcast_to(square[4:5, 0:128], (8, 128))
    inv = lax.rsqrt(square[0:1, :] / D + EPS)
    for j in range(rows // 128):
        part = slice(j * 128, (j + 1) * 128)
        column = jnp.transpose(jnp.broadcast_to(inv[:, part], (128, 128)), (1, 0))
        column = jnp.concatenate([column] * (width // 128), axis=1)
        gate = total[part, 0:width] * column
        up = total[part, width : 2 * width] * column
        inner[part, :] = (gate * (1.0 / (1.0 + jnp.exp(-gate))) * up).astype(BF)


def down_kernel(flag, i0, i1, i2, i3, u0, u1, v0, v1, out, weights, made, sems, out_sems):
    width = i0.shape[1]
    span = out.shape[1]

    def copies_of(n, ref):
        return [
            pltpu.make_async_copy(
                ref.at[pl.ds(span + j * width, width), :],
                weights.at[pl.ds(n * width, width), pl.ds(j * 2 * width, 2 * width)],
                sems.at[n, j],
            )
            for j in range(2)
        ]

    fetch(flag, (u0, u1), (v0, v1), copies_of, N_TP)
    inner = jnp.concatenate([i0[...], i1[...], i2[...], i3[...]], axis=1)
    for n in range(N_TP):
        for copy in copies_of(n, u0):
            copy.wait()
    done = []
    for j in range(4):
        cols = pl.ds(j * width, width)
        made[:, cols] = jnp.dot(inner, weights[:, cols], preferred_element_type=F32).astype(BF)
        done.append(pltpu.make_async_copy(made.at[:, cols], out.at[:, cols], out_sems.at[j]))
        done[-1].start()
    for copy in done:
        copy.wait()


def mix_kernel(ids, sums, hidden, returned, out):
    experts = sums.shape[0] - 8
    named, slot = slots_of(ids, experts)
    inv = lax.rsqrt(sums[experts : experts + 1, :] / D + EPS)
    logits = sums[0:experts, :] * inv
    picked = jnp.where(named, 1.0 / (1.0 + jnp.exp(-logits)), 0.0)
    share = picked / jnp.sum(picked, axis=0, keepdims=True)
    wide = spread(slot, share)
    high = wide.astype(BF)
    low = (wide - high.astype(F32)).astype(BF)
    rows = returned[...]
    dims = (((0,), (0,)), ((), ()))
    mixed = lax.dot_general(high, rows, dims, preferred_element_type=F32)
    mixed += lax.dot_general(low, rows, dims, preferred_element_type=F32)
    out[...] = (hidden[...].astype(F32) + mixed).astype(BF)


def body(resid, queries, keys, values, norm_gain, w_router, expert_ids, w_gate, w_up, w_down):
    tokens, width = resid.shape
    experts = lax.axis_size("ep")
    slots = experts * CAP
    units = w_gate.shape[2]
    sec, tp = lax.axis_index("sec"), lax.axis_index("tp")
    parity = (tp % 2).astype(jnp.int32).reshape(1)
    flag = (sec == tp // 2).astype(jnp.int32).reshape(1)
    ids = expert_ids.T
    gain = norm_gain.reshape(1, width)

    payload = struct((width + 2 * units, 2 * units), BF)
    dma = pltpu.SemaphoreType.DMA

    def pack(block, *after):
        return call(
            pack_kernel, payload, [SM] + [ANY] * (3 + len(after)), ANY, [dma((4,))],
            (0, 3_000_000), WHOLE_VMEM,
        )(block, w_gate, w_up, w_down, *after)

    stay, turn = [], []
    for s in range(2):
        for t in range(N_TP):
            here = s * N_TP + t
            if s == t // 2:
                stay.append((here, here))
            else:
                stay.append((here, (1 - s) * N_TP + (t + 2) % N_TP))
            if s == ((t + 1) % N_TP) // 2:
                turn.append((here, s * N_TP + (t + 1) % N_TP))
            else:
                turn.append((here, (1 - s) * N_TP + (t + 3) % N_TP))
    swap = [(0, 1), (1, 0)]
    u0 = lax.ppermute(pack(parity), ("sec", "tp"), stay)
    v0 = lax.ppermute(u0, "sec", swap)

    hidden, outgoing = call(
        lambda *refs: attention_kernel(experts, *refs),
        [struct((tokens, width), BF), struct((slots, width), BF)],
        [VM] * 5,
        [VM, ANY],
        [pltpu.VMEM((slots, width), BF), dma((4,))],
        (300_000_000, 2_500_000),
    )(ids, queries, keys, values, resid)
    arrived = lax.all_to_all(
        outgoing.reshape(experts, CAP, width), "ep", split_axis=0, concat_axis=0, tiled=True
    ).reshape(slots, width)

    u1 = lax.ppermute(pack(1 - parity, outgoing), ("sec", "tp"), turn)
    v1 = lax.ppermute(u1, "sec", swap)
    sums = call(
        router_kernel, struct((experts + 8, tokens), F32), [VM] * 3, VM, (), (150_000_000, 600_000)
    )(hidden, gain, w_router.T)

    lines = slots + 16 + experts // 2
    message = struct((N_TP, lines, 2 * units), BF)
    place = jnp.concatenate([flag] + [((tp - k) % N_TP).reshape(1) for k in range(N_TP)])
    partial = call(
        up_kernel,
        message,
        [SM, VM, VM, VM, ANY, ANY, ANY, ANY],
        ANY,
        [
            pltpu.VMEM((N_TP, width, 2 * units), BF),
            pltpu.VMEM((N_TP, lines, 2 * units), BF),
            dma((N_TP,)),
            dma((N_TP,)),
        ],
        (2_200_000_000, 8_000_000),
    )(place, arrived, gain, sums, u0, u1, v0, v1)
    got = lax.all_to_all(partial, "tp", split_axis=0, concat_axis=0, tiled=True)
    inner, sums = call(
        inner_kernel,
        [struct((slots, units), BF), struct((experts + 8, tokens), F32)],
        [VM],
        [VM, VM],
        (),
        (1_000_000, 2_500_000),
    )(got)
    inners = [inner] + [None] * 3
    for k in (2, 1, 3):
        inners[k] = lax.ppermute(inner, "tp", [(i, (i + k) % N_TP) for i in range(N_TP)])
    expert_out = call(
        down_kernel,
        struct((slots, width), BF),
        [SM, VM, VM, VM, VM, ANY, ANY, ANY, ANY],
        ANY,
        [
            pltpu.VMEM((N_TP * units, width), BF),
            pltpu.VMEM((slots, width), BF),
            dma((N_TP, 2)),
            dma((4,)),
        ],
        (1_100_000_000, 4_000_000),
    )(flag, *inners, u0, u1, v0, v1)
    returned = lax.all_to_all(
        expert_out.reshape(experts, CAP, width), "ep", split_axis=0, concat_axis=0, tiled=True
    ).reshape(slots, width)
    return call(mix_kernel, struct((tokens, width), BF), [VM] * 4, VM)(ids, sums, hidden, returned)


def solution(mesh):
    rows, cols = P(("sec", "ep"), "tp"), P(("sec", "ep"), None)
    return jax.shard_map(
        body,
        mesh=mesh,
        in_specs=(
            rows,
            rows,
            rows,
            rows,
            P("tp"),
            P("tp", None),
            cols,
            P("ep", "sec", "tp"),
            P("ep", "sec", "tp"),
            P("ep", "tp", "sec"),
        ),
        out_specs=rows,
        check_vma=False,
    )
```

```python
import math

import jax
import jax.numpy as jnp
from jax import lax
from jax.experimental import pallas as pl
from jax.experimental.pallas import tpu as pltpu
from jax.sharding import PartitionSpec as P

D = 4096
HEAD_DIM = 128
CAP = 8
N_TP = 4
EPS = 1e-06

BF = jnp.bfloat16
F32 = jnp.float32
HIGHEST = lax.Precision.HIGHEST
VMEM_BYTES = 28 * 1024 * 1024
WHOLE_VMEM = 63 * 1024 * 1024


def call(kernel, out_shape, in_specs, out_specs, scratch=(), cost=(0, 0), vmem=VMEM_BYTES):
    return pl.pallas_call(
        kernel,
        out_shape=out_shape,
        in_specs=in_specs,
        out_specs=out_specs,
        scratch_shapes=scratch,
        cost_estimate=pl.CostEstimate(flops=cost[0], bytes_accessed=cost[1], transcendentals=0),
        compiler_params=pltpu.CompilerParams(vmem_limit_bytes=vmem),
    )


VM = pl.BlockSpec(memory_space=pltpu.VMEM)
ANY = pl.BlockSpec(memory_space=pl.ANY)
SM = pl.BlockSpec(memory_space=pltpu.SMEM)


def struct(shape, dtype):
    return jax.ShapeDtypeStruct(shape, dtype)


def nt(a, b, precision=None):
    return lax.dot_general(
        a, b, (((1,), (1,)), ((), ())), precision=precision, preferred_element_type=F32
    )


def pack_copies(base, gate, up, down, out, sems):
    width, span = gate.shape[2], down.shape[2] // 2
    rows = pl.ds(base, span)
    pairs = [
        (gate.at[0, rows, :], out.at[pl.ds(0, span), pl.ds(0, width)]),
        (up.at[0, rows, :], out.at[pl.ds(0, span), pl.ds(width, width)]),
    ]
    for j in range(2):
        cols = pl.ds(pl.multiple_of(base + j * 2 * width, 2 * width), 2 * width)
        pairs.append((down.at[0, :, cols], out.at[pl.ds(span + j * width, width), :]))
    return [pltpu.make_async_copy(src, dst, sems.at[n]) for n, (src, dst) in enumerate(pairs)]


def slots_of(ids_ref, experts):
    tokens = ids_ref.shape[1]
    expert = lax.broadcasted_iota(jnp.int32, (experts, tokens), 0)
    named = (ids_ref[0:1, :] == expert) | (ids_ref[1:2, :] == expert)
    before = lax.broadcasted_iota(jnp.int32, (tokens, tokens), 0) < lax.broadcasted_iota(
        jnp.int32, (tokens, tokens), 1
    )
    rank = jnp.dot(named.astype(BF), before.astype(BF), preferred_element_type=F32)
    return named, jnp.where(named, rank, -1.0)


def spread(slot, value):
    experts, tokens = slot.shape
    turn = lax.broadcasted_iota(jnp.int32, (experts, CAP, tokens), 1).astype(F32)
    hit = slot[:, None, :] == turn
    return jnp.where(hit, value[:, None, :], 0.0).reshape(experts * CAP, tokens)


def front_kernel(experts, parity, ids, q_, k_, v_, resid_, gate, up, down,
                 hidden_, outgoing, first, second,
                 q, k, v, resid, hidden, rows, pack, sems, pack_sems, out_sems):
    tokens, width = q.shape
    loads = [
        pltpu.make_async_copy(src, dst, sems.at[n])
        for n, (src, dst) in enumerate(((q_, q), (k_, k), (v_, v), (resid_, resid)))
    ]
    loads_pack = []
    for turn in range(2):
        block = parity[0] if turn == 0 else 1 - parity[0]
        base = pl.multiple_of(block * (down.shape[2] // 2), down.shape[2] // 2)
        loads_pack.append(pack_copies(base, gate, up, down, pack.at[turn], pack_sems.at[turn]))
    for copy in loads + loads_pack[0] + loads_pack[1]:
        copy.start()
    scale = 1.0 / math.sqrt(HEAD_DIM)
    _, slot = slots_of(ids, experts)
    pick = spread(slot, jnp.ones_like(slot)).astype(BF)
    for copy in loads:
        copy.wait()
    stores = []

    def store(src, dst):
        stores.append(pltpu.make_async_copy(src, dst, out_sems.at[len(stores)]))
        stores[-1].start()

    for n in range(width // HEAD_DIM):
        cols = slice(n * HEAD_DIM, (n + 1) * HEAD_DIM)
        scores = nt(q[:, cols], k[:, cols]) * scale
        top = jnp.max(scores, axis=1, keepdims=True)
        e = jnp.exp(scores - top)
        weights = (e / jnp.sum(e, axis=1, keepdims=True)).astype(BF)
        attended = jnp.dot(weights, v[:, cols], preferred_element_type=F32)
        h = (resid[:, cols].astype(F32) + attended).astype(BF)
        hidden[:, cols] = h
        rows[:, cols] = jnp.dot(pick, h, preferred_element_type=F32).astype(BF)
        if n % 2 == 1:
            pair = pl.ds((n - 1) * HEAD_DIM, 2 * HEAD_DIM)
            store(rows.at[:, pair], outgoing.at[:, pair])
        if n in (2, 5):
            turn = n // 3
            for copy in loads_pack[turn]:
                copy.wait()
            store(pack.at[turn], (first, second)[turn])
    store(hidden, hidden_)
    for copy in stores:
        copy.wait()


def router_kernel(hidden, gain, router, out):
    h = hidden[...].astype(F32)
    experts = router.shape[0]
    out[0:experts, :] = nt(router[...], h * gain[...], HIGHEST)
    out[experts : experts + 8, :] = nt(jnp.ones((8, h.shape[1]), F32), h * h, HIGHEST)


def split(value):
    high = value.astype(BF)
    return high, (value - high.astype(F32)).astype(BF)


def up_kernel(place, x, gain, sums, u0, u1, v0, v1, after, out, weights, sems):
    rows, depth = x.shape
    loads = [
        pltpu.make_async_copy(ref.at[pl.ds(0, depth), :], weights.at[n], sems.at[n])
        for n, ref in enumerate((u0, u1, v0, v1))
    ]
    for copy in loads:
        copy.start()
    xf = x[...].astype(F32)
    xg = (xf * gain[...]).astype(BF)
    high, low = split(xf * xf)
    ones = jnp.ones((8, depth), BF)
    total = nt(ones, high) + nt(ones, low)
    experts = sums.shape[0] - 8
    tokens = jnp.concatenate([sums[experts : experts + 8, :]] * 4, axis=1)
    tile = lax.broadcasted_iota(jnp.int32, total.shape, 0)
    squares = jnp.concatenate(split(jnp.where(tile < 4, total, tokens)), axis=0)
    half = experts // 2
    parts = split(sums[0:experts, :])
    logits = jnp.concatenate(
        [part[i * half : (i + 1) * half, :] for part in parts for i in range(2)], axis=1
    )
    for n in range(N_TP):
        target = place[n]
        loads[n].wait()
        out[target, 0:rows, :] = jnp.dot(xg, weights[n], preferred_element_type=F32).astype(BF)
        out[target, rows : rows + 16, :] = squares
        out[target, rows + 16 : rows + 16 + half, :] = logits


def inner_kernel(got, inner, sums):
    rows, width = inner.shape[1:]
    half = sums.shape[0] // 2 - 4
    total = got[0, 0:rows, :].astype(F32)
    tail = got[0, rows:, :].astype(F32)
    for n in range(1, N_TP):
        total = total + got[n, 0:rows, :].astype(F32)
        tail = tail + got[n, rows:, :].astype(F32)
    square = tail[0:8, :] + tail[8:16, :]
    logits = tail[16 : 16 + half, :]
    logits = logits[:, 0:256] + logits[:, 256:512]
    sums[0:half, :] = logits[:, 0:128]
    sums[half : 2 * half, :] = logits[:, 128:256]
    sums[2 * half : 2 * half + 8, :] = jnp.broadcast_to(square[4:5, 0:128], (8, 128))
    inv = lax.rsqrt(square[0:1, :] / D + EPS)
    for j in range(rows // 128):
        part = slice(j * 128, (j + 1) * 128)
        column = jnp.transpose(jnp.broadcast_to(inv[:, part], (128, 128)), (1, 0))
        column = jnp.concatenate([column] * (width // 128), axis=1)
        gate = total[part, 0:width] * column
        up = total[part, width : 2 * width] * column
        act = (gate * (1.0 / (1.0 + jnp.exp(-gate))) * up).astype(BF)
        for n in range(N_TP):
            inner[n, part, :] = act


def down_kernel(place, inners, u0, u1, v0, v1, out, weights, sems):
    width, span = inners.shape[2], out.shape[1]
    loads = [
        pltpu.make_async_copy(ref.at[pl.ds(span, 2 * width), :], weights.at[n], sems.at[n])
        for n, ref in enumerate((u0, u1, v0, v1))
    ]
    for copy in loads:
        copy.start()
    parts = [inners[place[n]] for n in range(N_TP)]
    for copy in loads:
        copy.wait()
    for j in range(2):
        total = jnp.zeros((out.shape[0], 2 * width), F32)
        for n, part in enumerate(parts):
            rows = weights[n, j * width : (j + 1) * width, :]
            total += jnp.dot(part, rows, preferred_element_type=F32)
        out[:, j * 2 * width : (j + 1) * 2 * width] = total.astype(BF)


def mix_kernel(ids, sums, hidden, returned, out):
    experts = sums.shape[0] - 8
    named, slot = slots_of(ids, experts)
    inv = lax.rsqrt(sums[experts : experts + 1, :] / D + EPS)
    logits = sums[0:experts, :] * inv
    picked = jnp.where(named, 1.0 / (1.0 + jnp.exp(-logits)), 0.0)
    share = picked / jnp.sum(picked, axis=0, keepdims=True)
    wide = spread(slot, share)
    high = wide.astype(BF)
    low = (wide - high.astype(F32)).astype(BF)
    rows = returned[...]
    dims = (((0,), (0,)), ((), ()))
    mixed = lax.dot_general(high, rows, dims, preferred_element_type=F32)
    mixed += lax.dot_general(low, rows, dims, preferred_element_type=F32)
    out[...] = (hidden[...].astype(F32) + mixed).astype(BF)


def body(resid, queries, keys, values, norm_gain, w_router, expert_ids, w_gate, w_up, w_down):
    tokens, width = resid.shape
    experts = lax.axis_size("ep")
    slots = experts * CAP
    units = w_gate.shape[2]
    sec, tp = lax.axis_index("sec"), lax.axis_index("tp")
    parity = (tp % 2).astype(jnp.int32).reshape(1)
    ids = expert_ids.T
    gain = norm_gain.reshape(1, width)

    dma = pltpu.SemaphoreType.DMA
    payload = struct((width + 2 * units, 2 * units), BF)
    hidden, outgoing, first, second = call(
        lambda *refs: front_kernel(experts, *refs),
        [struct((tokens, width), BF), struct((slots, width), BF), payload, payload],
        [SM, VM] + [ANY] * 7,
        [ANY] * 4,
        [pltpu.VMEM((tokens, width), BF)] * 5
        + [pltpu.VMEM((slots, width), BF), pltpu.VMEM((2,) + payload.shape, BF)]
        + [dma((4,)), dma((2, 4)), dma((7,))],
        (300_000_000, 8_500_000),
        WHOLE_VMEM,
    )(parity, ids, queries, keys, values, resid, w_gate, w_up, w_down)

    stay, turn = [], []
    for s in range(2):
        for t in range(N_TP):
            here = s * N_TP + t
            if s == t // 2:
                stay.append((here, here))
            else:
                stay.append((here, (1 - s) * N_TP + (t + 2) % N_TP))
            if s == ((t + 1) % N_TP) // 2:
                turn.append((here, s * N_TP + (t + 1) % N_TP))
            else:
                turn.append((here, (1 - s) * N_TP + (t + 3) % N_TP))
    swap = [(0, 1), (1, 0)]
    u0 = lax.ppermute(first, ("sec", "tp"), stay)
    u1 = lax.ppermute(second, ("sec", "tp"), turn)
    weights = [u0, u1, lax.ppermute(u0, "sec", swap), lax.ppermute(u1, "sec", swap)]
    base = jnp.where(sec == tp // 2, tp, tp + 2)
    place = jnp.stack([(base - n) % N_TP for n in range(N_TP)]).astype(jnp.int32)

    arrived = lax.all_to_all(
        outgoing.reshape(experts, CAP, width), "ep", split_axis=0, concat_axis=0, tiled=True
    ).reshape(slots, width)

    sums = call(
        router_kernel, struct((experts + 8, tokens), F32), [VM] * 3, VM, (), (150_000_000, 600_000)
    )(hidden, gain, w_router.T)

    pairs = [(experts + i, experts + i // 8 * 8 + (i + 1) % 8) for i in range(experts)]
    after = lax.ppermute(arrived, ("sec", "ep"), pairs)
    message = struct((N_TP, slots + 16 + experts // 2, 2 * units), BF)
    partial = call(
        up_kernel,
        message,
        [SM] + [VM] * 3 + [ANY] * 5,
        VM,
        [pltpu.VMEM((N_TP, width, 2 * units), BF), dma((N_TP,))],
        (2_200_000_000, 8_000_000),
    )(place, arrived, gain, sums, *weights, after)
    got = lax.all_to_all(partial, "tp", split_axis=0, concat_axis=0, tiled=True)
    inner, sums = call(
        inner_kernel,
        [struct((N_TP, slots, units), BF), struct((experts + 8, tokens), F32)],
        [VM],
        [VM, VM],
        (),
        (1_000_000, 2_500_000),
    )(got)
    inners = lax.all_to_all(inner, "tp", split_axis=0, concat_axis=0, tiled=True)
    expert_out = call(
        down_kernel,
        struct((slots, width), BF),
        [SM, VM] + [ANY] * 4,
        VM,
        [pltpu.VMEM((N_TP, 2 * units, 2 * units), BF), dma((N_TP,))],
        (1_100_000_000, 4_000_000),
    )(place, inners, *weights)
    returned = lax.all_to_all(
        expert_out.reshape(experts, CAP, width), "ep", split_axis=0, concat_axis=0, tiled=True
    ).reshape(slots, width)
    return call(mix_kernel, struct((tokens, width), BF), [VM] * 4, VM)(ids, sums, hidden, returned)


def solution(mesh):
    rows, cols = P(("sec", "ep"), "tp"), P(("sec", "ep"), None)
    return jax.shard_map(
        body,
        mesh=mesh,
        in_specs=(
            rows,
            rows,
            rows,
            rows,
            P("tp"),
            P("tp", None),
            cols,
            P("ep", "sec", "tp"),
            P("ep", "sec", "tp"),
            P("ep", "tp", "sec"),
        ),
        out_specs=rows,
        check_vma=False,
    )
```

```python
import math

import jax
import jax.numpy as jnp
from jax import lax
from jax.experimental import pallas as pl
from jax.experimental.pallas import tpu as pltpu
from jax.sharding import PartitionSpec as P

D = 4096
HEAD_DIM = 128
CAP = 8
N_TP = 4
EPS = 1e-06

BF = jnp.bfloat16
F32 = jnp.float32
HIGHEST = lax.Precision.HIGHEST
VMEM_BYTES = 28 * 1024 * 1024
WHOLE_VMEM = 63 * 1024 * 1024


def call(
    kernel, out_shape, in_specs, out_specs, scratch=(), cost=(0, 0), vmem=VMEM_BYTES, aliases=None
):
    return pl.pallas_call(
        kernel,
        out_shape=out_shape,
        in_specs=in_specs,
        out_specs=out_specs,
        scratch_shapes=scratch,
        input_output_aliases=aliases or {},
        cost_estimate=pl.CostEstimate(flops=cost[0], bytes_accessed=cost[1], transcendentals=0),
        compiler_params=pltpu.CompilerParams(vmem_limit_bytes=vmem),
    )


VM = pl.BlockSpec(memory_space=pltpu.VMEM)
ANY = pl.BlockSpec(memory_space=pl.ANY)
SM = pl.BlockSpec(memory_space=pltpu.SMEM)


def struct(shape, dtype):
    return jax.ShapeDtypeStruct(shape, dtype)


def nt(a, b, precision=None):
    return lax.dot_general(
        a, b, (((1,), (1,)), ((), ())), precision=precision, preferred_element_type=F32
    )


def pack_copies(base, gate, up, down, out, sems):
    width, span = gate.shape[2], down.shape[2] // 2
    rows = pl.ds(base, span)
    pairs = [
        (gate.at[0, rows, :], out.at[pl.ds(0, span), pl.ds(0, width)]),
        (up.at[0, rows, :], out.at[pl.ds(0, span), pl.ds(width, width)]),
    ]
    for j in range(2):
        cols = pl.ds(pl.multiple_of(base + j * 2 * width, 2 * width), 2 * width)
        pairs.append((down.at[0, :, cols], out.at[pl.ds(span + j * width, width), :]))
    return [pltpu.make_async_copy(src, dst, sems.at[n]) for n, (src, dst) in enumerate(pairs)]


def slots_of(ids_ref, experts):
    tokens = ids_ref.shape[1]
    expert = lax.broadcasted_iota(jnp.int32, (experts, tokens), 0)
    named = (ids_ref[0:1, :] == expert) | (ids_ref[1:2, :] == expert)
    before = lax.broadcasted_iota(jnp.int32, (tokens, tokens), 0) < lax.broadcasted_iota(
        jnp.int32, (tokens, tokens), 1
    )
    rank = jnp.dot(named.astype(BF), before.astype(BF), preferred_element_type=F32)
    return named, jnp.where(named, rank, -1.0)


def spread(slot, value):
    experts, tokens = slot.shape
    turn = lax.broadcasted_iota(jnp.int32, (experts, CAP, tokens), 1).astype(F32)
    hit = slot[:, None, :] == turn
    return jnp.where(hit, value[:, None, :], 0.0).reshape(experts * CAP, tokens)


def pack_kernel(parity, gate, up, down, first, second, pack, sems, out_sems):
    span = down.shape[2] // 2
    loads = []
    for turn in range(2):
        block = parity[0] if turn == 0 else 1 - parity[0]
        base = pl.multiple_of(block * span, span)
        loads.append(pack_copies(base, gate, up, down, pack.at[turn], sems.at[turn]))
    for copy in loads[0] + loads[1]:
        copy.start()
    stores = []
    for turn, out in enumerate((first, second)):
        for copy in loads[turn]:
            copy.wait()
        stores.append(pltpu.make_async_copy(pack.at[turn], out, out_sems.at[turn]))
        stores[-1].start()
    for copy in stores:
        copy.wait()


def front_kernel(experts, ids, q_, k_, v_, resid_, hidden_, outgoing,
                 q, k, v, resid, hidden, rows, sems, out_sems):
    tokens, width = q.shape
    loads = [
        pltpu.make_async_copy(src, dst, sems.at[n])
        for n, (src, dst) in enumerate(((q_, q), (k_, k), (v_, v), (resid_, resid)))
    ]
    for copy in loads:
        copy.start()
    scale = 1.0 / math.sqrt(HEAD_DIM)
    _, slot = slots_of(ids, experts)
    pick = spread(slot, jnp.ones_like(slot)).astype(BF)
    for copy in loads:
        copy.wait()
    stores = []
    heads = width // HEAD_DIM
    for n in range(heads):
        cols = slice(n * HEAD_DIM, (n + 1) * HEAD_DIM)
        scores = nt(q[:, cols], k[:, cols]) * scale
        top = jnp.max(scores, axis=1, keepdims=True)
        e = jnp.exp(scores - top)
        weights = (e / jnp.sum(e, axis=1, keepdims=True)).astype(BF)
        attended = jnp.dot(weights, v[:, cols], preferred_element_type=F32)
        h = (resid[:, cols].astype(F32) + attended).astype(BF)
        hidden[:, cols] = h
        rows[:, cols] = jnp.dot(pick, h, preferred_element_type=F32).astype(BF)
        if (n + 1) % (heads // 2) == 0:
            part = pl.ds((n + 1) * HEAD_DIM - width // 2, width // 2)
            for src, dst in ((rows, outgoing), (hidden, hidden_)):
                stores.append(
                    pltpu.make_async_copy(
                        src.at[:, part], dst.at[:, part], out_sems.at[len(stores)]
                    )
                )
                stores[-1].start()
    for copy in stores:
        copy.wait()


def router_kernel(hidden, gain, router, out):
    h = hidden[...].astype(F32)
    experts = router.shape[0]
    out[0:experts, :] = nt(router[...], h * gain[...], HIGHEST)
    out[experts : experts + 8, :] = nt(jnp.ones((8, h.shape[1]), F32), h * h, HIGHEST)


def split(value):
    high = value.astype(BF)
    return high, (value - high.astype(F32)).astype(BF)


def start_either(place, yes, no):
    @pl.when(place[N_TP] == 1)
    def _():
        for copy in yes:
            copy.start()

    @pl.when(place[N_TP] != 1)
    def _():
        for copy in no:
            copy.start()


def up_kernel(place, x, gain, sums, u0, u1, first, v0, v1, out, columns,
              xg, weights, sems, column_sems):
    rows, depth = x.shape
    units = weights.shape[2] // 2

    def load(n, ref):
        return pltpu.make_async_copy(ref.at[pl.ds(0, depth), :], weights.at[n], sems.at[n])

    def load_columns(n, j, ref):
        return pltpu.make_async_copy(
            ref.at[pl.ds(depth + j * units, units), :],
            columns.at[pl.ds(n * units, units), pl.ds(2 * j * units, 2 * units)],
            column_sems.at[n, j],
        )

    for n, ref in ((0, u0), (1, u1), (3, v1)):
        load(n, ref).start()
    start_either(place, [load(2, first)], [load(2, v0)])
    for j in range(2):
        for n, ref in ((0, u0), (1, u1), (3, v1)):
            load_columns(n, j, ref).start()
        start_either(place, [load_columns(2, j, first)], [load_columns(2, j, v0)])
    xf = x[...].astype(F32)
    xg[...] = (xf * gain[...]).astype(BF)
    partial = jnp.zeros((rows, 128), F32)
    for j in range(depth // 128):
        part = xf[:, j * 128 : (j + 1) * 128]
        partial += part * part
    high, low = split(partial)
    ones = jnp.ones((8, 128), BF)
    total = nt(ones, high) + nt(ones, low)
    experts = sums.shape[0] - 8
    tokens = jnp.concatenate([sums[experts : experts + 8, :]] * 4, axis=1)
    tile = lax.broadcasted_iota(jnp.int32, total.shape, 0)
    squares = jnp.concatenate(split(jnp.where(tile < 4, total, tokens)), axis=0)
    half = experts // 2
    parts = split(sums[0:experts, :])
    logits = jnp.concatenate(
        [part[i * half : (i + 1) * half, :] for part in parts for i in range(2)], axis=1
    )
    for n in range(N_TP):
        out[n, rows : rows + 16, :] = squares
        out[n, rows + 16 : rows + 16 + half, :] = logits
    for n in (0, 1, 3, 2):
        load(n, v1).wait()
        product = jnp.dot(xg[...], weights[n], preferred_element_type=F32)
        out[place[n], 0:rows, :] = product.astype(BF)
    for j in range(2):
        for n in range(N_TP):
            load_columns(n, j, v1).wait()


def after_kernel(message, after, out):
    pass


def inner_kernel(got, inner, sums):
    rows, width = inner.shape[1:]
    half = sums.shape[0] // 2 - 4
    total = got[0, 0:rows, :].astype(F32)
    tail = got[0, rows:, :].astype(F32)
    for n in range(1, N_TP):
        total = total + got[n, 0:rows, :].astype(F32)
        tail = tail + got[n, rows:, :].astype(F32)
    square = tail[0:8, :] + tail[8:16, :]
    logits = tail[16 : 16 + half, :]
    logits = logits[:, 0:256] + logits[:, 256:512]
    sums[0:half, :] = logits[:, 0:128]
    sums[half : 2 * half, :] = logits[:, 128:256]
    sums[2 * half : 2 * half + 8, :] = jnp.broadcast_to(square[4:5, 0:128], (8, 128))
    inv = lax.rsqrt(square[0:1, :] / D + EPS)
    for j in range(rows // 128):
        part = slice(j * 128, (j + 1) * 128)
        column = jnp.transpose(jnp.broadcast_to(inv[:, part], (128, 128)), (1, 0))
        column = jnp.concatenate([column] * (width // 128), axis=1)
        gate = total[part, 0:width] * column
        up = total[part, width : 2 * width] * column
        act = (gate * (1.0 / (1.0 + jnp.exp(-gate))) * up).astype(BF)
        for n in range(N_TP):
            inner[n, part, :] = act


def down_kernel(place, inners, columns, out, inner):
    width = inners.shape[2]
    for n in range(N_TP):
        inner[:, n * width : (n + 1) * width] = inners[place[n]]
    out[...] = jnp.dot(inner[...], columns[...], preferred_element_type=F32).astype(BF)


def mix_kernel(ids, sums, hidden, returned, out):
    experts = sums.shape[0] - 8
    named, slot = slots_of(ids, experts)
    inv = lax.rsqrt(sums[experts : experts + 1, :] / D + EPS)
    logits = sums[0:experts, :] * inv
    picked = jnp.where(named, 1.0 / (1.0 + jnp.exp(-logits)), 0.0)
    share = picked / jnp.sum(picked, axis=0, keepdims=True)
    wide = spread(slot, share)
    high = wide.astype(BF)
    low = (wide - high.astype(F32)).astype(BF)
    rows = returned[...]
    dims = (((0,), (0,)), ((), ()))
    mixed = lax.dot_general(high, rows, dims, preferred_element_type=F32)
    mixed += lax.dot_general(low, rows, dims, preferred_element_type=F32)
    out[...] = (hidden[...].astype(F32) + mixed).astype(BF)


def body(resid, queries, keys, values, norm_gain, w_router, expert_ids, w_gate, w_up, w_down):
    tokens, width = resid.shape
    experts = lax.axis_size("ep")
    slots = experts * CAP
    units = w_gate.shape[2]
    sec, tp = lax.axis_index("sec"), lax.axis_index("tp")
    parity = (tp % 2).astype(jnp.int32).reshape(1)
    ids = expert_ids.T
    gain = norm_gain.reshape(1, width)

    dma = pltpu.SemaphoreType.DMA
    payload = struct((width + 2 * units, 2 * units), BF)
    first, second = call(
        pack_kernel,
        [payload, payload],
        [SM] + [ANY] * 3,
        [ANY] * 2,
        [pltpu.VMEM((2,) + payload.shape, BF), dma((2, 4)), dma((2,))],
        (0, 6_000_000),
        WHOLE_VMEM,
    )(parity, w_gate, w_up, w_down)
    hidden, outgoing = call(
        lambda *refs: front_kernel(experts, *refs),
        [struct((tokens, width), BF), struct((slots, width), BF)],
        [VM] + [ANY] * 4,
        [ANY] * 2,
        [pltpu.VMEM((tokens, width), BF)] * 5
        + [pltpu.VMEM((slots, width), BF), dma((4,)), dma((4,))],
        (300_000_000, 3_000_000),
        WHOLE_VMEM,
    )(ids, queries, keys, values, resid)
    sums = call(
        router_kernel, struct((experts + 8, tokens), F32), [VM] * 3, VM, (), (150_000_000, 600_000)
    )(hidden, gain, w_router.T)

    near = [(t // 2, t) for t in range(N_TP)]

    def index(s, t):
        return s * N_TP + t % N_TP

    stay, turn, over = [], [], []
    for s in range(2):
        for t in range(N_TP):
            here = index(s, t)
            stay.append((here, index(1 - s, t) if (s, t) in near else index(s, t + 2)))
            odd = s == ((t + 1) % N_TP) // 2
            turn.append((here, index(s, t + 1) if odd else index(1 - s, t + 3)))
            if (s, t) in near:
                over.append((here, index(1 - s, t)))
    both = ("sec", "tp")
    u0, u1 = lax.ppermute(first, both, stay), lax.ppermute(second, both, turn)
    u1 = call(after_kernel, payload, [ANY, ANY], ANY, aliases={0: 0})(u1, sums)
    v0, v1 = lax.ppermute(u0, both, over), lax.ppermute(u1, "sec", [(0, 1), (1, 0)])
    weights = [u0, u1, first, v0, v1]
    is_near = sec == tp // 2
    back = jnp.where(is_near, jnp.array([2, 1, 0, 3]), jnp.array([0, 3, 2, 1]))
    place = jnp.append((tp - back) % N_TP, is_near).astype(jnp.int32)

    arrived = lax.all_to_all(
        outgoing.reshape(experts, CAP, width), "ep", split_axis=0, concat_axis=0, tiled=True
    ).reshape(slots, width)

    pairs = [(experts + i, experts + i // 8 * 8 + (i + 1) % 8) for i in range(experts)]
    after = lax.ppermute(arrived, ("sec", "ep"), pairs)
    message = struct((N_TP, slots + 16 + experts // 2, 2 * units), BF)
    partial, columns = call(
        up_kernel,
        [message, struct((N_TP * units, width), BF)],
        [SM] + [VM] * 3 + [ANY] * 5,
        [VM, VM],
        [
            pltpu.VMEM((slots, width), BF),
            pltpu.VMEM((N_TP, width, 2 * units), BF),
            dma((N_TP,)),
            dma((N_TP, 2)),
        ],
        (2_200_000_000, 9_000_000),
    )(place, arrived, gain, sums, *weights)
    partial = call(after_kernel, message, [VM, ANY], VM, aliases={0: 0})(partial, after)
    got = lax.all_to_all(partial, "tp", split_axis=0, concat_axis=0, tiled=True)
    inner, sums = call(
        inner_kernel,
        [struct((N_TP, slots, units), BF), struct((experts + 8, tokens), F32)],
        [VM],
        [VM, VM],
        (),
        (1_000_000, 2_500_000),
    )(got)
    inners = lax.all_to_all(inner, "tp", split_axis=0, concat_axis=0, tiled=True)
    expert_out = call(
        down_kernel,
        struct((slots, width), BF),
        [SM, VM, VM],
        VM,
        [pltpu.VMEM((slots, N_TP * units), BF)],
        (1_100_000_000, 4_000_000),
    )(place, inners, columns)
    returned = lax.all_to_all(
        expert_out.reshape(experts, CAP, width), "ep", split_axis=0, concat_axis=0, tiled=True
    ).reshape(slots, width)
    return call(mix_kernel, struct((tokens, width), BF), [VM] * 4, VM)(ids, sums, hidden, returned)


def solution(mesh):
    rows, cols = P(("sec", "ep"), "tp"), P(("sec", "ep"), None)
    return jax.shard_map(
        body,
        mesh=mesh,
        in_specs=(
            rows,
            rows,
            rows,
            rows,
            P("tp"),
            P("tp", None),
            cols,
            P("ep", "sec", "tp"),
            P("ep", "sec", "tp"),
            P("ep", "tp", "sec"),
        ),
        out_specs=rows,
        check_vma=False,
    )
```

```python
import math

import jax
import jax.numpy as jnp
from jax import lax
from jax.experimental import pallas as pl
from jax.experimental.pallas import tpu as pltpu
from jax.sharding import PartitionSpec as P

D = 4096
HEAD_DIM = 128
CAP = 8
N_TP = 4
EPS = 1e-06

BF = jnp.bfloat16
F32 = jnp.float32
HIGHEST = lax.Precision.HIGHEST
VMEM_BYTES = 28 * 1024 * 1024
WHOLE_VMEM = 63 * 1024 * 1024


def call(
    kernel, out_shape, in_specs, out_specs, scratch=(), cost=(0, 0), vmem=VMEM_BYTES, aliases=None
):
    return pl.pallas_call(
        kernel,
        out_shape=out_shape,
        in_specs=in_specs,
        out_specs=out_specs,
        scratch_shapes=scratch,
        input_output_aliases=aliases or {},
        cost_estimate=pl.CostEstimate(flops=cost[0], bytes_accessed=cost[1], transcendentals=0),
        compiler_params=pltpu.CompilerParams(vmem_limit_bytes=vmem),
    )


VM = pl.BlockSpec(memory_space=pltpu.VMEM)
ANY = pl.BlockSpec(memory_space=pl.ANY)
SM = pl.BlockSpec(memory_space=pltpu.SMEM)


def struct(shape, dtype):
    return jax.ShapeDtypeStruct(shape, dtype)


def nt(a, b, precision=None):
    return lax.dot_general(
        a, b, (((1,), (1,)), ((), ())), precision=precision, preferred_element_type=F32
    )


def pack_copies(base, gate, up, down, out, sems):
    width, span = gate.shape[2], down.shape[2] // 2
    rows = pl.ds(base, span)
    pairs = [
        (gate.at[0, rows, :], out.at[pl.ds(0, span), pl.ds(0, width)]),
        (up.at[0, rows, :], out.at[pl.ds(0, span), pl.ds(width, width)]),
    ]
    for j in range(2):
        cols = pl.ds(pl.multiple_of(base + j * 2 * width, 2 * width), 2 * width)
        pairs.append((down.at[0, :, cols], out.at[pl.ds(span + j * width, width), :]))
    return [pltpu.make_async_copy(src, dst, sems.at[n]) for n, (src, dst) in enumerate(pairs)]


def slots_of(ids_ref, experts):
    tokens = ids_ref.shape[1]
    expert = lax.broadcasted_iota(jnp.int32, (experts, tokens), 0)
    named = (ids_ref[0:1, :] == expert) | (ids_ref[1:2, :] == expert)
    before = lax.broadcasted_iota(jnp.int32, (tokens, tokens), 0) < lax.broadcasted_iota(
        jnp.int32, (tokens, tokens), 1
    )
    rank = jnp.dot(named.astype(BF), before.astype(BF), preferred_element_type=F32)
    return named, jnp.where(named, rank, -1.0)


def spread(slot, value):
    experts, tokens = slot.shape
    turn = lax.broadcasted_iota(jnp.int32, (experts, CAP, tokens), 1).astype(F32)
    hit = slot[:, None, :] == turn
    return jnp.where(hit, value[:, None, :], 0.0).reshape(experts * CAP, tokens)


def pack_kernel(parity, gate, up, down, first, second, pack, sems, out_sems):
    span = down.shape[2] // 2
    loads = []
    for turn in range(2):
        block = parity[0] if turn == 0 else 1 - parity[0]
        base = pl.multiple_of(block * span, span)
        loads.append(pack_copies(base, gate, up, down, pack.at[turn], sems.at[turn]))
    for copy in loads[0] + loads[1]:
        copy.start()
    stores = []
    for turn, out in enumerate((first, second)):
        for copy in loads[turn]:
            copy.wait()
        stores.append(pltpu.make_async_copy(pack.at[turn], out, out_sems.at[turn]))
        stores[-1].start()
    for copy in stores:
        copy.wait()


def front_kernel(experts, ids, q_, k_, v_, resid_, hidden_, outgoing,
                 q, k, v, resid, hidden, rows, sems, out_sems):
    tokens, width = q.shape
    loads = [
        pltpu.make_async_copy(src, dst, sems.at[n])
        for n, (src, dst) in enumerate(((q_, q), (k_, k), (v_, v), (resid_, resid)))
    ]
    for copy in loads:
        copy.start()
    scale = 1.0 / math.sqrt(HEAD_DIM)
    _, slot = slots_of(ids, experts)
    pick = spread(slot, jnp.ones_like(slot)).astype(BF)
    for copy in loads:
        copy.wait()
    stores = []
    heads = width // HEAD_DIM
    for n in range(heads):
        cols = slice(n * HEAD_DIM, (n + 1) * HEAD_DIM)
        scores = nt(q[:, cols], k[:, cols]) * scale
        top = jnp.max(scores, axis=1, keepdims=True)
        e = jnp.exp(scores - top)
        weights = (e / jnp.sum(e, axis=1, keepdims=True)).astype(BF)
        attended = jnp.dot(weights, v[:, cols], preferred_element_type=F32)
        h = (resid[:, cols].astype(F32) + attended).astype(BF)
        hidden[:, cols] = h
        rows[:, cols] = jnp.dot(pick, h, preferred_element_type=F32).astype(BF)
        if (n + 1) % (heads // 2) == 0:
            part = pl.ds((n + 1) * HEAD_DIM - width // 2, width // 2)
            for src, dst in ((rows, outgoing), (hidden, hidden_)):
                stores.append(
                    pltpu.make_async_copy(
                        src.at[:, part], dst.at[:, part], out_sems.at[len(stores)]
                    )
                )
                stores[-1].start()
    for copy in stores:
        copy.wait()


def router_kernel(hidden, gain, router, out):
    h = hidden[...].astype(F32)
    experts = router.shape[0]
    out[0:experts, :] = nt(router[...], h * gain[...], HIGHEST)
    out[experts : experts + 8, :] = nt(jnp.ones((8, h.shape[1]), F32), h * h, HIGHEST)


def split(value):
    high = value.astype(BF)
    return high, (value - high.astype(F32)).astype(BF)


def start_either(place, yes, no):
    @pl.when(place[N_TP] == 1)
    def _():
        for copy in yes:
            copy.start()

    @pl.when(place[N_TP] != 1)
    def _():
        for copy in no:
            copy.start()


def up_kernel(place, x, gain, sums, u0, u1, first, v0, v1, out, columns, head,
              xg, weights, sems, column_sems):
    rows, depth = x.shape
    units = weights.shape[2] // 2

    def load(n, ref):
        return pltpu.make_async_copy(ref.at[pl.ds(0, depth), :], weights.at[n], sems.at[n])

    def load_columns(n, j, ref):
        return pltpu.make_async_copy(
            ref.at[pl.ds(depth + j * units, units), :],
            columns.at[pl.ds(n * units, units), pl.ds(2 * j * units, 2 * units)],
            column_sems.at[n, j],
        )

    for n, ref in ((0, u0), (1, u1), (3, v1)):
        load(n, ref).start()
    start_either(place, [load(2, first)], [load(2, v0)])
    for j in range(2):
        for n, ref in ((0, u0), (1, u1), (3, v1)):
            load_columns(n, j, ref).start()
        start_either(place, [load_columns(2, j, first)], [load_columns(2, j, v0)])
    xf = x[...].astype(F32)
    xg[...] = (xf * gain[...]).astype(BF)
    head[...] = x[0 : head.shape[0], :]
    partial = jnp.zeros((rows, 128), F32)
    for j in range(depth // 128):
        part = xf[:, j * 128 : (j + 1) * 128]
        partial += part * part
    high, low = split(partial)
    ones = jnp.ones((8, 128), BF)
    total = nt(ones, high) + nt(ones, low)
    experts = sums.shape[0] - 8
    tokens = jnp.concatenate([sums[experts : experts + 8, :]] * 4, axis=1)
    tile = lax.broadcasted_iota(jnp.int32, total.shape, 0)
    squares = jnp.concatenate(split(jnp.where(tile < 4, total, tokens)), axis=0)
    quarter = experts // 4
    logits = jnp.concatenate(
        [sums[i * quarter : (i + 1) * quarter, :].astype(BF) for i in range(4)], axis=1
    )
    for n in range(N_TP):
        out[n, rows : rows + 16, :] = squares
        out[n, rows + 16 : rows + 16 + quarter, :] = logits
    for n in (0, 1, 3, 2):
        load(n, v1).wait()
        product = jnp.dot(xg[...], weights[n], preferred_element_type=F32)
        out[place[n], 0:rows, :] = product.astype(BF)
    for j in range(2):
        for n in range(N_TP):
            load_columns(n, j, v1).wait()


def after_kernel(message, after, out):
    pass


def inner_kernel(got, inner, sums):
    rows, width = inner.shape[1:]
    quarter = sums.shape[0] // 4 - 2
    total = got[0, 0:rows, :].astype(F32)
    tail = got[0, rows:, :].astype(F32)
    for n in range(1, N_TP):
        total = total + got[n, 0:rows, :].astype(F32)
        tail = tail + got[n, rows:, :].astype(F32)
    square = tail[0:8, :] + tail[8:16, :]
    for i in range(4):
        lanes = slice(i * 128, (i + 1) * 128)
        sums[i * quarter : (i + 1) * quarter, :] = tail[16 : 16 + quarter, lanes]
    sums[4 * quarter : 4 * quarter + 8, :] = jnp.broadcast_to(square[4:5, 0:128], (8, 128))
    inv = lax.rsqrt(square[0:1, :] / D + EPS)
    for j in range(rows // 128):
        part = slice(j * 128, (j + 1) * 128)
        column = jnp.transpose(jnp.broadcast_to(inv[:, part], (128, 128)), (1, 0))
        column = jnp.concatenate([column] * (width // 128), axis=1)
        gate = total[part, 0:width] * column
        up = total[part, width : 2 * width] * column
        act = (gate * (1.0 / (1.0 + jnp.exp(-gate))) * up).astype(BF)
        for n in range(N_TP):
            inner[n, part, :] = act


def down_kernel(place, inners, columns, out, inner):
    width = inners.shape[2]
    for n in range(N_TP):
        inner[:, n * width : (n + 1) * width] = inners[place[n]]
    out[...] = jnp.dot(inner[...], columns[...], preferred_element_type=F32).astype(BF)


def mix_kernel(ids, sums, hidden, returned, out):
    experts = sums.shape[0] - 8
    named, slot = slots_of(ids, experts)
    inv = lax.rsqrt(sums[experts : experts + 1, :] / D + EPS)
    logits = sums[0:experts, :] * inv
    picked = jnp.where(named, 1.0 / (1.0 + jnp.exp(-logits)), 0.0)
    share = picked / jnp.sum(picked, axis=0, keepdims=True)
    wide = spread(slot, share)
    high = wide.astype(BF)
    low = (wide - high.astype(F32)).astype(BF)
    rows = returned[...]
    dims = (((0,), (0,)), ((), ()))
    mixed = lax.dot_general(high, rows, dims, preferred_element_type=F32)
    mixed += lax.dot_general(low, rows, dims, preferred_element_type=F32)
    out[...] = (hidden[...].astype(F32) + mixed).astype(BF)


def second_only(experts, step):
    return [(experts + i, experts + i // 8 * 8 + (i + step) % 8) for i in range(experts)]


def body(resid, queries, keys, values, norm_gain, w_router, expert_ids, w_gate, w_up, w_down):
    tokens, width = resid.shape
    experts = lax.axis_size("ep")
    slots = experts * CAP
    units = w_gate.shape[2]
    sec, tp = lax.axis_index("sec"), lax.axis_index("tp")
    parity = (tp % 2).astype(jnp.int32).reshape(1)
    ids = expert_ids.T
    gain = norm_gain.reshape(1, width)

    dma = pltpu.SemaphoreType.DMA
    payload = struct((width + 2 * units, 2 * units), BF)
    first, second = call(
        pack_kernel,
        [payload, payload],
        [SM] + [ANY] * 3,
        [ANY] * 2,
        [pltpu.VMEM((2,) + payload.shape, BF), dma((2, 4)), dma((2,))],
        (0, 6_000_000),
        WHOLE_VMEM,
    )(parity, w_gate, w_up, w_down)
    hidden, outgoing = call(
        lambda *refs: front_kernel(experts, *refs),
        [struct((tokens, width), BF), struct((slots, width), BF)],
        [VM] + [ANY] * 4,
        [ANY] * 2,
        [pltpu.VMEM((tokens, width), BF)] * 5
        + [pltpu.VMEM((slots, width), BF), dma((4,)), dma((4,))],
        (300_000_000, 3_000_000),
        WHOLE_VMEM,
    )(ids, queries, keys, values, resid)
    sums = call(
        router_kernel, struct((experts + 8, tokens), F32), [VM] * 3, VM, (), (150_000_000, 600_000)
    )(hidden, gain, w_router.T)

    near = [(t // 2, t) for t in range(N_TP)]

    def index(s, t):
        return s * N_TP + t % N_TP

    stay, turn, over = [], [], []
    for s in range(2):
        for t in range(N_TP):
            here = index(s, t)
            stay.append((here, index(1 - s, t) if (s, t) in near else index(s, t + 2)))
            odd = s == ((t + 1) % N_TP) // 2
            turn.append((here, index(s, t + 1) if odd else index(1 - s, t + 3)))
            if (s, t) in near:
                over.append((here, index(1 - s, t)))
    both = ("sec", "tp")
    u0, u1 = lax.ppermute(first, both, stay), lax.ppermute(second, both, turn)
    u1 = call(after_kernel, payload, [ANY, ANY], ANY, aliases={0: 0})(u1, sums)
    v0, v1 = lax.ppermute(u0, both, over), lax.ppermute(u1, "sec", [(0, 1), (1, 0)])
    weights = [u0, u1, first, v0, v1]
    is_near = sec == tp // 2
    back = jnp.where(is_near, jnp.array([2, 1, 0, 3]), jnp.array([0, 3, 2, 1]))
    place = jnp.append((tp - back) % N_TP, is_near).astype(jnp.int32)

    after = lax.ppermute(hidden, ("sec", "ep"), second_only(experts, 1))
    outgoing = call(
        after_kernel, struct((slots, width), BF), [ANY, ANY], ANY, vmem=WHOLE_VMEM, aliases={0: 0}
    )(outgoing, after)
    arrived = lax.all_to_all(
        outgoing.reshape(experts, CAP, width), "ep", split_axis=0, concat_axis=0, tiled=True
    ).reshape(slots, width)

    message = struct((N_TP, slots + 16 + experts // 4, 2 * units), BF)
    partial, columns, head = call(
        up_kernel,
        [message, struct((N_TP * units, width), BF), struct((tokens, width), BF)],
        [SM] + [VM] * 3 + [ANY] * 5,
        [VM, VM, VM],
        [
            pltpu.VMEM((slots, width), BF),
            pltpu.VMEM((N_TP, width, 2 * units), BF),
            dma((N_TP,)),
            dma((N_TP, 2)),
        ],
        (2_200_000_000, 9_000_000),
    )(place, arrived, gain, sums, *weights)
    after = lax.ppermute(head, ("sec", "ep"), second_only(experts, 1))
    partial = call(after_kernel, message, [VM, ANY], VM, aliases={0: 0})(partial, after)
    got = lax.all_to_all(partial, "tp", split_axis=0, concat_axis=0, tiled=True)
    inner, sums = call(
        inner_kernel,
        [struct((N_TP, slots, units), BF), struct((experts + 8, tokens), F32)],
        [VM],
        [VM, VM],
        (),
        (1_000_000, 2_500_000),
    )(got)
    inners = lax.all_to_all(inner, "tp", split_axis=0, concat_axis=0, tiled=True)
    expert_out = call(
        down_kernel,
        struct((slots, width), BF),
        [SM, VM, VM],
        VM,
        [pltpu.VMEM((slots, N_TP * units), BF)],
        (1_100_000_000, 4_000_000),
    )(place, inners, columns)
    returned = lax.all_to_all(
        expert_out.reshape(experts, CAP, width), "ep", split_axis=0, concat_axis=0, tiled=True
    ).reshape(slots, width)
    return call(mix_kernel, struct((tokens, width), BF), [VM] * 4, VM)(ids, sums, hidden, returned)


def solution(mesh):
    rows, cols = P(("sec", "ep"), "tp"), P(("sec", "ep"), None)
    return jax.shard_map(
        body,
        mesh=mesh,
        in_specs=(
            rows,
            rows,
            rows,
            rows,
            P("tp"),
            P("tp", None),
            cols,
            P("ep", "sec", "tp"),
            P("ep", "sec", "tp"),
            P("ep", "tp", "sec"),
        ),
        out_specs=rows,
        check_vma=False,
    )
```

```python
import math

import jax
import jax.numpy as jnp
from jax import lax
from jax.experimental import pallas as pl
from jax.experimental.pallas import tpu as pltpu
from jax.sharding import PartitionSpec as P

D = 4096
HEAD_DIM = 128
CAP = 8
N_TP = 4
EPS = 1e-06

BF = jnp.bfloat16
F32 = jnp.float32
HIGHEST = lax.Precision.HIGHEST
VMEM_BYTES = 28 * 1024 * 1024
WHOLE_VMEM = 63 * 1024 * 1024


def call(
    kernel, out_shape, in_specs, out_specs, scratch=(), cost=(0, 0), vmem=VMEM_BYTES, aliases=None
):
    return pl.pallas_call(
        kernel,
        out_shape=out_shape,
        in_specs=in_specs,
        out_specs=out_specs,
        scratch_shapes=scratch,
        input_output_aliases=aliases or {},
        cost_estimate=pl.CostEstimate(flops=cost[0], bytes_accessed=cost[1], transcendentals=0),
        compiler_params=pltpu.CompilerParams(vmem_limit_bytes=vmem),
    )


VM = pl.BlockSpec(memory_space=pltpu.VMEM)
ANY = pl.BlockSpec(memory_space=pl.ANY)
SM = pl.BlockSpec(memory_space=pltpu.SMEM)


def struct(shape, dtype):
    return jax.ShapeDtypeStruct(shape, dtype)


def nt(a, b, precision=None):
    return lax.dot_general(
        a, b, (((1,), (1,)), ((), ())), precision=precision, preferred_element_type=F32
    )


def pack_copies(base, gate, up, down, out, sems):
    width, span = gate.shape[2], down.shape[2] // 2
    rows = pl.ds(base, span)
    pairs = [
        (gate.at[0, rows, :], out.at[pl.ds(0, span), pl.ds(0, width)]),
        (up.at[0, rows, :], out.at[pl.ds(0, span), pl.ds(width, width)]),
    ]
    for j in range(2):
        cols = pl.ds(pl.multiple_of(base + j * 2 * width, 2 * width), 2 * width)
        pairs.append((down.at[0, :, cols], out.at[pl.ds(span + j * width, width), :]))
    return [pltpu.make_async_copy(src, dst, sems.at[n]) for n, (src, dst) in enumerate(pairs)]


def slots_of(ids_ref, experts):
    tokens = ids_ref.shape[1]
    expert = lax.broadcasted_iota(jnp.int32, (experts, tokens), 0)
    named = (ids_ref[0:1, :] == expert) | (ids_ref[1:2, :] == expert)
    before = lax.broadcasted_iota(jnp.int32, (tokens, tokens), 0) < lax.broadcasted_iota(
        jnp.int32, (tokens, tokens), 1
    )
    rank = jnp.dot(named.astype(BF), before.astype(BF), preferred_element_type=F32)
    return named, jnp.where(named, rank, -1.0)


def spread(slot, value):
    experts, tokens = slot.shape
    turn = lax.broadcasted_iota(jnp.int32, (experts, CAP, tokens), 1).astype(F32)
    hit = slot[:, None, :] == turn
    return jnp.where(hit, value[:, None, :], 0.0).reshape(experts * CAP, tokens)


def pack_kernel(parity, gate, up, down, first, second, pack, sems, out_sems):
    span = down.shape[2] // 2
    loads = []
    for turn in range(2):
        block = parity[0] if turn == 0 else 1 - parity[0]
        base = pl.multiple_of(block * span, span)
        loads.append(pack_copies(base, gate, up, down, pack.at[turn], sems.at[turn]))
    for copy in loads[0] + loads[1]:
        copy.start()
    stores = []
    for turn, out in enumerate((first, second)):
        for copy in loads[turn]:
            copy.wait()
        stores.append(pltpu.make_async_copy(pack.at[turn], out, out_sems.at[turn]))
        stores[-1].start()
    for copy in stores:
        copy.wait()


def front_kernel(experts, ids, q_, k_, v_, resid_, hidden_, outgoing,
                 q, k, v, resid, hidden, rows, sems, out_sems):
    tokens, width = q.shape
    loads = [
        pltpu.make_async_copy(src, dst, sems.at[n])
        for n, (src, dst) in enumerate(((q_, q), (k_, k), (v_, v), (resid_, resid)))
    ]
    for copy in loads:
        copy.start()
    scale = 1.0 / math.sqrt(HEAD_DIM)
    _, slot = slots_of(ids, experts)
    pick = spread(slot, jnp.ones_like(slot)).astype(BF)
    for copy in loads:
        copy.wait()
    stores = []
    heads = width // HEAD_DIM
    for n in range(heads):
        cols = slice(n * HEAD_DIM, (n + 1) * HEAD_DIM)
        scores = nt(q[:, cols], k[:, cols]) * scale
        top = jnp.max(scores, axis=1, keepdims=True)
        e = jnp.exp(scores - top)
        weights = (e / jnp.sum(e, axis=1, keepdims=True)).astype(BF)
        attended = jnp.dot(weights, v[:, cols], preferred_element_type=F32)
        h = (resid[:, cols].astype(F32) + attended).astype(BF)
        hidden[:, cols] = h
        rows[:, cols] = jnp.dot(pick, h, preferred_element_type=F32).astype(BF)
        if (n + 1) % (heads // 2) == 0:
            part = pl.ds((n + 1) * HEAD_DIM - width // 2, width // 2)
            for src, dst in ((rows, outgoing), (hidden, hidden_)):
                stores.append(
                    pltpu.make_async_copy(
                        src.at[:, part], dst.at[:, part], out_sems.at[len(stores)]
                    )
                )
                stores[-1].start()
    for copy in stores:
        copy.wait()


def router_kernel(hidden, gain, router, out):
    h = hidden[...].astype(F32)
    experts = router.shape[0]
    out[0:experts, :] = nt(router[...], h * gain[...], HIGHEST)
    out[experts : experts + 8, :] = nt(jnp.ones((8, h.shape[1]), F32), h * h, HIGHEST)


def split(value):
    high = value.astype(BF)
    return high, (value - high.astype(F32)).astype(BF)


def start_either(place, yes, no):
    @pl.when(place[N_TP] == 1)
    def _():
        for copy in yes:
            copy.start()

    @pl.when(place[N_TP] != 1)
    def _():
        for copy in no:
            copy.start()


def up_kernel(place, x, gain, sums, u0, u1, first, v0, v1, out, columns, head,
              xg, weights, sems, column_sems):
    rows, depth = x.shape
    units = weights.shape[2] // 2

    def load(n, ref):
        return pltpu.make_async_copy(ref.at[pl.ds(0, depth), :], weights.at[n], sems.at[n])

    def load_columns(n, j, ref):
        return pltpu.make_async_copy(
            ref.at[pl.ds(depth + j * units, units), :],
            columns.at[pl.ds(n * units, units), pl.ds(2 * j * units, 2 * units)],
            column_sems.at[n, j],
        )

    for n, ref in ((0, u0), (1, u1), (3, v1)):
        load(n, ref).start()
    start_either(place, [load(2, first)], [load(2, v0)])
    for j in range(2):
        for n, ref in ((0, u0), (1, u1), (3, v1)):
            load_columns(n, j, ref).start()
        start_either(place, [load_columns(2, j, first)], [load_columns(2, j, v0)])
    xf = x[...].astype(F32)
    xg[...] = (xf * gain[...]).astype(BF)
    head[...] = x[0 : head.shape[0], :]
    partial = jnp.zeros((rows, 128), F32)
    for j in range(depth // 128):
        part = xf[:, j * 128 : (j + 1) * 128]
        partial += part * part
    high, low = split(partial)
    ones = jnp.ones((8, 128), BF)
    total = nt(ones, high) + nt(ones, low)
    experts = sums.shape[0] - 8
    tokens = jnp.concatenate([sums[experts : experts + 8, :]] * 4, axis=1)
    tile = lax.broadcasted_iota(jnp.int32, total.shape, 0)
    squares = jnp.concatenate(split(jnp.where(tile < 4, total, tokens)), axis=0)
    quarter = experts // 4
    logits = jnp.concatenate(
        [sums[i * quarter : (i + 1) * quarter, :].astype(BF) for i in range(4)], axis=1
    )
    for n in range(N_TP):
        out[n, rows : rows + 16, :] = squares
        out[n, rows + 16 : rows + 16 + quarter, :] = logits
    for n in (0, 1, 3, 2):
        load(n, v1).wait()
        product = jnp.dot(xg[...], weights[n], preferred_element_type=F32)
        out[place[n], 0:rows, :] = product.astype(BF)
    for j in range(2):
        for n in range(N_TP):
            load_columns(n, j, v1).wait()


def after_kernel(message, after, out):
    pass


def inner_kernel(got, inner, sums):
    rows, width = inner.shape[1:]
    quarter = sums.shape[0] // 4 - 2
    total = got[0, 0:rows, :].astype(F32)
    tail = got[0, rows:, :].astype(F32)
    for n in range(1, N_TP):
        total = total + got[n, 0:rows, :].astype(F32)
        tail = tail + got[n, rows:, :].astype(F32)
    square = tail[0:8, :] + tail[8:16, :]
    for i in range(4):
        lanes = slice(i * 128, (i + 1) * 128)
        sums[i * quarter : (i + 1) * quarter, :] = tail[16 : 16 + quarter, lanes]
    sums[4 * quarter : 4 * quarter + 8, :] = jnp.broadcast_to(square[4:5, 0:128], (8, 128))
    inv = lax.rsqrt(square[0:1, :] / D + EPS)
    for j in range(rows // 128):
        part = slice(j * 128, (j + 1) * 128)
        column = jnp.transpose(jnp.broadcast_to(inv[:, part], (128, 128)), (1, 0))
        column = jnp.concatenate([column] * (width // 128), axis=1)
        gate = total[part, 0:width] * column
        up = total[part, width : 2 * width] * column
        act = (gate * (1.0 / (1.0 + jnp.exp(-gate))) * up).astype(BF)
        for n in range(N_TP):
            inner[n, part, :] = act


def down_kernel(place, inners, columns, out, inner):
    width = inners.shape[2]
    for n in range(N_TP):
        inner[:, n * width : (n + 1) * width] = inners[place[n]]
    out[...] = jnp.dot(inner[...], columns[...], preferred_element_type=F32).astype(BF)


def mix_kernel(ids, sums, hidden, returned, out):
    experts = sums.shape[0] - 8
    named, slot = slots_of(ids, experts)
    inv = lax.rsqrt(sums[experts : experts + 1, :] / D + EPS)
    logits = sums[0:experts, :] * inv
    negative = jnp.where(named, jnp.minimum(logits, 0.0), -1e30)
    negative = negative - jnp.max(negative, axis=0, keepdims=True)
    picked = jnp.where(named, jnp.exp(negative) / (1.0 + jnp.exp(-jnp.abs(logits))), 0.0)
    share = picked / jnp.sum(picked, axis=0, keepdims=True)
    wide = spread(slot, share)
    high = wide.astype(BF)
    low = (wide - high.astype(F32)).astype(BF)
    rows = returned[...]
    dims = (((0,), (0,)), ((), ()))
    mixed = lax.dot_general(high, rows, dims, preferred_element_type=F32)
    mixed += lax.dot_general(low, rows, dims, preferred_element_type=F32)
    out[...] = (hidden[...].astype(F32) + mixed).astype(BF)


def second_only(experts, step):
    return [(experts + i, experts + i // 8 * 8 + (i + step) % 8) for i in range(experts)]


def body(resid, queries, keys, values, norm_gain, w_router, expert_ids, w_gate, w_up, w_down):
    tokens, width = resid.shape
    experts = lax.axis_size("ep")
    slots = experts * CAP
    units = w_gate.shape[2]
    sec, tp = lax.axis_index("sec"), lax.axis_index("tp")
    parity = (tp % 2).astype(jnp.int32).reshape(1)
    ids = expert_ids.T
    gain = norm_gain.reshape(1, width)

    dma = pltpu.SemaphoreType.DMA
    payload = struct((width + 2 * units, 2 * units), BF)
    first, second = call(
        pack_kernel,
        [payload, payload],
        [SM] + [ANY] * 3,
        [ANY] * 2,
        [pltpu.VMEM((2,) + payload.shape, BF), dma((2, 4)), dma((2,))],
        (0, 6_000_000),
        WHOLE_VMEM,
    )(parity, w_gate, w_up, w_down)
    hidden, outgoing = call(
        lambda *refs: front_kernel(experts, *refs),
        [struct((tokens, width), BF), struct((slots, width), BF)],
        [VM] + [ANY] * 4,
        [ANY] * 2,
        [pltpu.VMEM((tokens, width), BF)] * 5
        + [pltpu.VMEM((slots, width), BF), dma((4,)), dma((4,))],
        (300_000_000, 3_000_000),
        WHOLE_VMEM,
    )(ids, queries, keys, values, resid)
    sums = call(
        router_kernel, struct((experts + 8, tokens), F32), [VM] * 3, VM, (), (150_000_000, 600_000)
    )(hidden, gain, w_router.T)

    near = [(t // 2, t) for t in range(N_TP)]

    def index(s, t):
        return s * N_TP + t % N_TP

    stay, turn, over = [], [], []
    for s in range(2):
        for t in range(N_TP):
            here = index(s, t)
            stay.append((here, index(1 - s, t) if (s, t) in near else index(s, t + 2)))
            odd = s == ((t + 1) % N_TP) // 2
            turn.append((here, index(s, t + 1) if odd else index(1 - s, t + 3)))
            if (s, t) in near:
                over.append((here, index(1 - s, t)))
    both = ("sec", "tp")
    u0, u1 = lax.ppermute(first, both, stay), lax.ppermute(second, both, turn)
    u1 = call(after_kernel, payload, [ANY, ANY], ANY, aliases={0: 0})(u1, sums)
    v0, v1 = lax.ppermute(u0, both, over), lax.ppermute(u1, "sec", [(0, 1), (1, 0)])
    weights = [u0, u1, first, v0, v1]
    is_near = sec == tp // 2
    back = jnp.where(is_near, jnp.array([2, 1, 0, 3]), jnp.array([0, 3, 2, 1]))
    place = jnp.append((tp - back) % N_TP, is_near).astype(jnp.int32)

    after = lax.ppermute(hidden, ("sec", "ep"), second_only(experts, 1))
    outgoing = call(
        after_kernel, struct((slots, width), BF), [ANY, ANY], ANY, vmem=WHOLE_VMEM, aliases={0: 0}
    )(outgoing, after)
    arrived = lax.all_to_all(
        outgoing.reshape(experts, CAP, width), "ep", split_axis=0, concat_axis=0, tiled=True
    ).reshape(slots, width)

    message = struct((N_TP, slots + 16 + experts // 4, 2 * units), BF)
    partial, columns, head = call(
        up_kernel,
        [message, struct((N_TP * units, width), BF), struct((tokens, width), BF)],
        [SM] + [VM] * 3 + [ANY] * 5,
        [VM, VM, VM],
        [
            pltpu.VMEM((slots, width), BF),
            pltpu.VMEM((N_TP, width, 2 * units), BF),
            dma((N_TP,)),
            dma((N_TP, 2)),
        ],
        (2_200_000_000, 9_000_000),
    )(place, arrived, gain, sums, *weights)
    after = lax.ppermute(head, ("sec", "ep"), second_only(experts, 1))
    partial = call(after_kernel, message, [VM, ANY], VM, aliases={0: 0})(partial, after)
    got = lax.all_to_all(partial, "tp", split_axis=0, concat_axis=0, tiled=True)
    inner, sums = call(
        inner_kernel,
        [struct((N_TP, slots, units), BF), struct((experts + 8, tokens), F32)],
        [VM],
        [VM, VM],
        (),
        (1_000_000, 2_500_000),
    )(got)
    inners = lax.all_to_all(inner, "tp", split_axis=0, concat_axis=0, tiled=True)
    expert_out = call(
        down_kernel,
        struct((slots, width), BF),
        [SM, VM, VM],
        VM,
        [pltpu.VMEM((slots, N_TP * units), BF)],
        (1_100_000_000, 4_000_000),
    )(place, inners, columns)
    returned = lax.all_to_all(
        expert_out.reshape(experts, CAP, width), "ep", split_axis=0, concat_axis=0, tiled=True
    ).reshape(slots, width)
    return call(mix_kernel, struct((tokens, width), BF), [VM] * 4, VM)(ids, sums, hidden, returned)


def solution(mesh):
    rows, cols = P(("sec", "ep"), "tp"), P(("sec", "ep"), None)
    return jax.shard_map(
        body,
        mesh=mesh,
        in_specs=(
            rows,
            rows,
            rows,
            rows,
            P("tp"),
            P("tp", None),
            cols,
            P("ep", "sec", "tp"),
            P("ep", "sec", "tp"),
            P("ep", "tp", "sec"),
        ),
        out_specs=rows,
        check_vma=False,
    )
```

```python
import math

import jax
import jax.numpy as jnp
from jax import lax
from jax.experimental import pallas as pl
from jax.experimental.pallas import tpu as pltpu
from jax.sharding import PartitionSpec as P

D = 4096
HEAD_DIM = 128
CAP = 8
N_TP = 4
EPS = 1e-06

BF = jnp.bfloat16
F32 = jnp.float32
HIGHEST = lax.Precision.HIGHEST
VMEM_BYTES = 28 * 1024 * 1024
WHOLE_VMEM = 63 * 1024 * 1024


def call(
    kernel, out_shape, in_specs, out_specs, scratch=(), cost=(0, 0), vmem=VMEM_BYTES, aliases=None
):
    return pl.pallas_call(
        kernel,
        out_shape=out_shape,
        in_specs=in_specs,
        out_specs=out_specs,
        scratch_shapes=scratch,
        input_output_aliases=aliases or {},
        cost_estimate=pl.CostEstimate(flops=cost[0], bytes_accessed=cost[1], transcendentals=0),
        compiler_params=pltpu.CompilerParams(vmem_limit_bytes=vmem),
    )


VM = pl.BlockSpec(memory_space=pltpu.VMEM)
ANY = pl.BlockSpec(memory_space=pl.ANY)
SM = pl.BlockSpec(memory_space=pltpu.SMEM)


def struct(shape, dtype):
    return jax.ShapeDtypeStruct(shape, dtype)


def nt(a, b, precision=None):
    return lax.dot_general(
        a, b, (((1,), (1,)), ((), ())), precision=precision, preferred_element_type=F32
    )


def pack_copies(base, gate, up, down, out, sems):
    width, span = gate.shape[2], down.shape[2] // 2
    rows = pl.ds(base, span)
    pairs = [
        (gate.at[0, rows, :], out.at[pl.ds(0, span), pl.ds(0, width)]),
        (up.at[0, rows, :], out.at[pl.ds(0, span), pl.ds(width, width)]),
    ]
    for j in range(2):
        cols = pl.ds(pl.multiple_of(base + j * 2 * width, 2 * width), 2 * width)
        pairs.append((down.at[0, :, cols], out.at[pl.ds(span + j * width, width), :]))
    return [pltpu.make_async_copy(src, dst, sems.at[n]) for n, (src, dst) in enumerate(pairs)]


def slots_of(ids_ref, experts):
    tokens = ids_ref.shape[1]
    expert = lax.broadcasted_iota(jnp.int32, (experts, tokens), 0)
    named = (ids_ref[0:1, :] == expert) | (ids_ref[1:2, :] == expert)
    before = lax.broadcasted_iota(jnp.int32, (tokens, tokens), 0) < lax.broadcasted_iota(
        jnp.int32, (tokens, tokens), 1
    )
    rank = jnp.dot(named.astype(BF), before.astype(BF), preferred_element_type=F32)
    return named, jnp.where(named, rank, -1.0)


def spread(slot, value):
    experts, tokens = slot.shape
    turn = lax.broadcasted_iota(jnp.int32, (experts, CAP, tokens), 1).astype(F32)
    hit = slot[:, None, :] == turn
    return jnp.where(hit, value[:, None, :], 0.0).reshape(experts * CAP, tokens)


def pack_kernel(parity, gate, up, down, first, second, pack, sems, out_sems):
    span = down.shape[2] // 2
    loads = []
    for turn in range(2):
        block = parity[0] if turn == 0 else 1 - parity[0]
        base = pl.multiple_of(block * span, span)
        loads.append(pack_copies(base, gate, up, down, pack.at[turn], sems.at[turn]))
    for copy in loads[0] + loads[1]:
        copy.start()
    stores = []
    for turn, out in enumerate((first, second)):
        for copy in loads[turn]:
            copy.wait()
        stores.append(pltpu.make_async_copy(pack.at[turn], out, out_sems.at[turn]))
        stores[-1].start()
    for copy in stores:
        copy.wait()


def front_kernel(experts, ids, q_, k_, v_, resid_, hidden_, outgoing,
                 q, k, v, resid, hidden, rows, sems, out_sems):
    tokens, width = q.shape
    loads = [
        pltpu.make_async_copy(src, dst, sems.at[n])
        for n, (src, dst) in enumerate(((q_, q), (k_, k), (v_, v), (resid_, resid)))
    ]
    for copy in loads:
        copy.start()
    scale = 1.0 / math.sqrt(HEAD_DIM)
    _, slot = slots_of(ids, experts)
    pick = spread(slot, jnp.ones_like(slot)).astype(BF)
    for copy in loads:
        copy.wait()
    stores = []
    heads = width // HEAD_DIM
    for n in range(heads):
        cols = slice(n * HEAD_DIM, (n + 1) * HEAD_DIM)
        scores = nt(q[:, cols], k[:, cols]) * scale
        top = jnp.max(scores, axis=1, keepdims=True)
        e = jnp.exp(scores - top)
        weights = (e * (1.0 / jnp.sum(e, axis=1, keepdims=True))).astype(BF)
        attended = jnp.dot(weights, v[:, cols], preferred_element_type=F32)
        h = (resid[:, cols].astype(F32) + attended).astype(BF)
        hidden[:, cols] = h
        rows[:, cols] = jnp.dot(pick, h, preferred_element_type=F32).astype(BF)
        if (n + 1) % (heads // 2) == 0:
            part = pl.ds((n + 1) * HEAD_DIM - width // 2, width // 2)
            for src, dst in ((rows, outgoing), (hidden, hidden_)):
                stores.append(
                    pltpu.make_async_copy(
                        src.at[:, part], dst.at[:, part], out_sems.at[len(stores)]
                    )
                )
                stores[-1].start()
    for copy in stores:
        copy.wait()


def router_kernel(hidden, gain, router, out):
    h = hidden[...].astype(F32)
    experts = router.shape[0]
    out[0:experts, :] = nt(router[...], h * gain[...], HIGHEST)
    out[experts : experts + 8, :] = nt(jnp.ones((8, h.shape[1]), F32), h * h, HIGHEST)


def split(value):
    high = value.astype(BF)
    return high, (value - high.astype(F32)).astype(BF)


def start_either(place, yes, no):
    @pl.when(place[N_TP] == 1)
    def _():
        for copy in yes:
            copy.start()

    @pl.when(place[N_TP] != 1)
    def _():
        for copy in no:
            copy.start()


def up_kernel(place, x, gain, sums, u0, u1, first, v0, v1, out, columns, head,
              xg, weights, sems, column_sems):
    rows, depth = x.shape
    units = weights.shape[2] // 2

    def load(n, ref):
        return pltpu.make_async_copy(ref.at[pl.ds(0, depth), :], weights.at[n], sems.at[n])

    def load_columns(n, j, ref):
        return pltpu.make_async_copy(
            ref.at[pl.ds(depth + j * units, units), :],
            columns.at[pl.ds(n * units, units), pl.ds(2 * j * units, 2 * units)],
            column_sems.at[n, j],
        )

    for n, ref in ((0, u0), (1, u1), (3, v1)):
        load(n, ref).start()
    start_either(place, [load(2, first)], [load(2, v0)])
    for j in range(2):
        for n, ref in ((0, u0), (1, u1), (3, v1)):
            load_columns(n, j, ref).start()
        start_either(place, [load_columns(2, j, first)], [load_columns(2, j, v0)])
    xf = x[...].astype(F32)
    xg[...] = (xf * gain[...]).astype(BF)
    head[...] = x[0 : head.shape[0], :]
    partial = jnp.zeros((rows, 128), F32)
    for j in range(depth // 128):
        part = xf[:, j * 128 : (j + 1) * 128]
        partial += part * part
    high, low = split(partial)
    ones = jnp.ones((8, 128), BF)
    total = nt(ones, high) + nt(ones, low)
    experts = sums.shape[0] - 8
    tokens = jnp.concatenate([sums[experts : experts + 8, :]] * 4, axis=1)
    tile = lax.broadcasted_iota(jnp.int32, total.shape, 0)
    squares = jnp.concatenate(split(jnp.where(tile < 4, total, tokens)), axis=0)
    quarter = experts // 4
    logits = jnp.concatenate(
        [sums[i * quarter : (i + 1) * quarter, :].astype(BF) for i in range(4)], axis=1
    )
    for n in range(N_TP):
        out[n, rows : rows + 16, :] = squares
        out[n, rows + 16 : rows + 16 + quarter, :] = logits
    for n in (0, 1, 3, 2):
        load(n, v1).wait()
        product = jnp.dot(xg[...], weights[n], preferred_element_type=F32)
        out[place[n], 0:rows, :] = product.astype(BF)
    for j in range(2):
        for n in range(N_TP):
            load_columns(n, j, v1).wait()


def after_kernel(message, after, out):
    pass


def inner_kernel(got, inner, sums):
    rows, width = inner.shape[1:]
    quarter = sums.shape[0] // 4 - 2
    total = got[0, 0:rows, :].astype(F32)
    tail = got[0, rows:, :].astype(F32)
    for n in range(1, N_TP):
        total = total + got[n, 0:rows, :].astype(F32)
        tail = tail + got[n, rows:, :].astype(F32)
    square = tail[0:8, :] + tail[8:16, :]
    for i in range(4):
        lanes = slice(i * 128, (i + 1) * 128)
        sums[i * quarter : (i + 1) * quarter, :] = tail[16 : 16 + quarter, lanes]
    sums[4 * quarter : 4 * quarter + 8, :] = jnp.broadcast_to(square[4:5, 0:128], (8, 128))
    inv = lax.rsqrt(square[0:1, :] / D + EPS)
    for j in range(rows // 128):
        part = slice(j * 128, (j + 1) * 128)
        column = jnp.transpose(jnp.broadcast_to(inv[:, part], (128, 128)), (1, 0))
        column = jnp.concatenate([column] * (width // 128), axis=1)
        gate = total[part, 0:width] * column
        up = total[part, width : 2 * width] * column
        act = (gate * (1.0 / (1.0 + jnp.exp(-gate))) * up).astype(BF)
        for n in range(N_TP):
            inner[n, part, :] = act


def down_kernel(place, inners, columns, out, inner):
    width = inners.shape[2]
    for n in range(N_TP):
        inner[:, n * width : (n + 1) * width] = inners[place[n]]
    out[...] = jnp.dot(inner[...], columns[...], preferred_element_type=F32).astype(BF)


def mix_kernel(ids, sums, hidden, returned, out):
    experts = sums.shape[0] - 8
    named, slot = slots_of(ids, experts)
    inv = lax.rsqrt(sums[experts : experts + 1, :] / D + EPS)
    logits = sums[0:experts, :] * inv
    negative = jnp.where(named, jnp.minimum(logits, 0.0), -1e30)
    negative = negative - jnp.max(negative, axis=0, keepdims=True)
    picked = jnp.where(named, jnp.exp(negative) / (1.0 + jnp.exp(-jnp.abs(logits))), 0.0)
    share = picked / jnp.sum(picked, axis=0, keepdims=True)
    wide = spread(slot, share)
    high = wide.astype(BF)
    low = (wide - high.astype(F32)).astype(BF)
    both = jnp.concatenate([high, low], axis=1)
    dims = (((0,), (0,)), ((), ()))
    mixed = lax.dot_general(both, returned[...], dims, preferred_element_type=F32)
    tokens = hidden.shape[0]
    mixed = mixed[0:tokens, :] + mixed[tokens:, :]
    out[...] = (hidden[...].astype(F32) + mixed).astype(BF)


def second_only(experts, step):
    return [(experts + i, experts + i // 8 * 8 + (i + step) % 8) for i in range(experts)]


def body(resid, queries, keys, values, norm_gain, w_router, expert_ids, w_gate, w_up, w_down):
    tokens, width = resid.shape
    experts = lax.axis_size("ep")
    slots = experts * CAP
    units = w_gate.shape[2]
    sec, tp = lax.axis_index("sec"), lax.axis_index("tp")
    parity = (tp % 2).astype(jnp.int32).reshape(1)
    ids = expert_ids.T
    gain = norm_gain.reshape(1, width)

    dma = pltpu.SemaphoreType.DMA
    payload = struct((width + 2 * units, 2 * units), BF)
    first, second = call(
        pack_kernel,
        [payload, payload],
        [SM] + [ANY] * 3,
        [ANY] * 2,
        [pltpu.VMEM((2,) + payload.shape, BF), dma((2, 4)), dma((2,))],
        (0, 6_000_000),
        WHOLE_VMEM,
    )(parity, w_gate, w_up, w_down)
    hidden, outgoing = call(
        lambda *refs: front_kernel(experts, *refs),
        [struct((tokens, width), BF), struct((slots, width), BF)],
        [VM] + [ANY] * 4,
        [ANY] * 2,
        [pltpu.VMEM((tokens, width), BF)] * 5
        + [pltpu.VMEM((slots, width), BF), dma((4,)), dma((4,))],
        (300_000_000, 3_000_000),
        WHOLE_VMEM,
    )(ids, queries, keys, values, resid)
    sums = call(
        router_kernel, struct((experts + 8, tokens), F32), [VM] * 3, VM, (), (150_000_000, 600_000)
    )(hidden, gain, w_router.T)

    near = [(t // 2, t) for t in range(N_TP)]

    def index(s, t):
        return s * N_TP + t % N_TP

    stay, turn, over = [], [], []
    for s in range(2):
        for t in range(N_TP):
            here = index(s, t)
            stay.append((here, index(1 - s, t) if (s, t) in near else index(s, t + 2)))
            odd = s == ((t + 1) % N_TP) // 2
            turn.append((here, index(s, t + 1) if odd else index(1 - s, t + 3)))
            if (s, t) in near:
                over.append((here, index(1 - s, t)))
    both = ("sec", "tp")
    u0, u1 = lax.ppermute(first, both, stay), lax.ppermute(second, both, turn)
    u1 = call(after_kernel, payload, [ANY, ANY], ANY, aliases={0: 0})(u1, sums)
    v0, v1 = lax.ppermute(u0, both, over), lax.ppermute(u1, "sec", [(0, 1), (1, 0)])
    weights = [u0, u1, first, v0, v1]
    is_near = sec == tp // 2
    back = jnp.where(is_near, jnp.array([2, 1, 0, 3]), jnp.array([0, 3, 2, 1]))
    place = jnp.append((tp - back) % N_TP, is_near).astype(jnp.int32)

    after = lax.ppermute(hidden, ("sec", "ep"), second_only(experts, 1))
    outgoing = call(
        after_kernel, struct((slots, width), BF), [ANY, ANY], ANY, vmem=WHOLE_VMEM, aliases={0: 0}
    )(outgoing, after)
    arrived = lax.all_to_all(
        outgoing.reshape(experts, CAP, width), "ep", split_axis=0, concat_axis=0, tiled=True
    ).reshape(slots, width)

    message = struct((N_TP, slots + 16 + experts // 4, 2 * units), BF)
    partial, columns, head = call(
        up_kernel,
        [message, struct((N_TP * units, width), BF), struct((tokens, width), BF)],
        [SM] + [VM] * 3 + [ANY] * 5,
        [VM, VM, VM],
        [
            pltpu.VMEM((slots, width), BF),
            pltpu.VMEM((N_TP, width, 2 * units), BF),
            dma((N_TP,)),
            dma((N_TP, 2)),
        ],
        (2_200_000_000, 9_000_000),
    )(place, arrived, gain, sums, *weights)
    after = lax.ppermute(head, ("sec", "ep"), second_only(experts, 1))
    partial = call(after_kernel, message, [VM, ANY], VM, aliases={0: 0})(partial, after)
    got = lax.all_to_all(partial, "tp", split_axis=0, concat_axis=0, tiled=True)
    inner, sums = call(
        inner_kernel,
        [struct((N_TP, slots, units), BF), struct((experts + 8, tokens), F32)],
        [VM],
        [VM, VM],
        (),
        (1_000_000, 2_500_000),
    )(got)
    inners = lax.all_to_all(inner, "tp", split_axis=0, concat_axis=0, tiled=True)
    expert_out = call(
        down_kernel,
        struct((slots, width), BF),
        [SM, VM, VM],
        VM,
        [pltpu.VMEM((slots, N_TP * units), BF)],
        (1_100_000_000, 4_000_000),
    )(place, inners, columns)
    returned = lax.all_to_all(
        expert_out.reshape(experts, CAP, width), "ep", split_axis=0, concat_axis=0, tiled=True
    ).reshape(slots, width)
    return call(mix_kernel, struct((tokens, width), BF), [VM] * 4, VM)(ids, sums, hidden, returned)


def solution(mesh):
    rows, cols = P(("sec", "ep"), "tp"), P(("sec", "ep"), None)
    return jax.shard_map(
        body,
        mesh=mesh,
        in_specs=(
            rows,
            rows,
            rows,
            rows,
            P("tp"),
            P("tp", None),
            cols,
            P("ep", "sec", "tp"),
            P("ep", "sec", "tp"),
            P("ep", "tp", "sec"),
        ),
        out_specs=rows,
        check_vma=False,
    )
```
